32 devices in a mesh: section: 4 (over y, x), dp: 8 (over z, core).
Axes of the slice: x: 2, y: 2, z: 4, core: 2. Of those that a mesh axis runs over, the one named last changes fastest.
Arguments:
- visible: bfloat16 [32, 49, 768], P(('section', 'dp')), may hold values from -6 to 6
- cotangent: bfloat16 [32, 196, 512], P(('section', 'dp')), may hold values from -6 to 6
- keep_index: int32 [32, 49], P(('section', 'dp')), may hold values from 0 to 195, as said below
- positions: float32 [196, 512], replicated, may hold values from -1 to 1
- enc_qkv: float32 [768, 2304], P('dp', 'section'), may hold values from -0.21875 to 0.21875
- enc_out: float32 [768, 768], P('dp', 'section'), may hold values from -0.4375 to 0.4375
- enc_up: float32 [768, 3072], P('dp', 'section'), may hold values from -0.21875 to 0.21875
- enc_down: float32 [3072, 768], P('dp', 'section'), may hold values from -0.109375 to 0.109375
- dec_embed: float32 [768, 512], P('dp', 'section'), may hold values from -0.21875 to 0.21875
- dec_qkv: float32 [512, 1536], P('dp', 'section'), may hold values from -0.25 to 0.25
- dec_out: float32 [512, 512], P('dp', 'section'), may hold values from -0.75 to 0.75
- dec_up: float32 [512, 2048], P('dp', 'section'), may hold values from -0.25 to 0.25
- dec_down: float32 [2048, 512], P('dp', 'section'), may hold values from -0.125 to 0.125
- enc_gains: float32 [2, 768], P(None, ('section', 'dp')), may hold values from 0.5 to 1.5
- enc_biases: float32 [6, 768], P(None, ('section', 'dp')), may hold values from -1.2 to 1.2
- enc_up_bias: float32 [3072], P(('section', 'dp')), may hold values from -1.2 to 1.2
- dec_gains: float32 [2, 512], P(None, ('section', 'dp')), may hold values from 0.5 to 1.5
- dec_biases: float32 [8, 512], P(None, ('section', 'dp')), may hold values from -1.2 to 1.2
- dec_up_bias: float32 [2048], P(('section', 'dp')), may hold values from -1.2 to 1.2
Outputs:
- block_out: float32 [32, 196, 512], P(('section', 'dp'))
- input_grad: float32 [32, 49, 768], P(('section', 'dp'))
- grad_enc_qkv: float32 [768, 2304], P('dp', 'section')
- grad_enc_out: float32 [768, 768], P('dp', 'section')
- grad_enc_up: float32 [768, 3072], P('dp', 'section')
- grad_enc_down: float32 [3072, 768], P('dp', 'section')
- grad_dec_embed: float32 [768, 512], P('dp', 'section')
- grad_dec_qkv: float32 [512, 1536], P('dp', 'section')
- grad_dec_out: float32 [512, 512], P('dp', 'section')
- grad_dec_up: float32 [512, 2048], P('dp', 'section')
- grad_dec_down: float32 [2048, 512], P('dp', 'section')
- grad_enc_gains: float32 [2, 768], P(None, ('section', 'dp'))
- grad_enc_biases: float32 [6, 768], P(None, ('section', 'dp'))
- grad_enc_up_bias: float32 [3072], P(('section', 'dp'))
- grad_dec_gains: float32 [2, 512], P(None, ('section', 'dp'))
- grad_dec_biases: float32 [8, 512], P(None, ('section', 'dp'))
- grad_dec_up_bias: float32 [2048], P(('section', 'dp'))
The draws below stay inside these ranges and needn't reach their ends.
Inputs may be any that keep to these rules, and one draw needn't show every extreme that they name: Each row of keep_index holds 49 different patch positions of the 196 of an image.
All inputs are finite; a program needn't handle non-finite values.
Results may differ from the reference program's by a relative error of at most 0.02.
Values may be sent and summed in bfloat16 or wider, within the bound.
No kernel may reach another device: no remote copies, remote signals or barrier semaphores. Data moves between devices by JAX's collectives and lax.ppermute only.
A program may use at most 576 MiB of HBM per device.

```python
import jax
import jax.numpy as jnp
from jax import lax

DE = 768
HE = 12
FE = 3072
DD = 512
HD = 16
FD = 2048
PATCHES = 196
KEEP = 49
IMAGES = 32


def draw_keep_index(key, part):
    scores = jax.random.randint(key, (IMAGES, PATCHES), 0, 1 << 20) * 256 + jnp.arange(PATCHES, dtype=jnp.int32)[None, :]
    scores = scores.at[0, PATCHES - 1].set(-1)
    scores = scores.at[IMAGES - 1, 0].set(-1)
    ranking = jnp.argsort(scores, axis=1, stable=True)
    return ranking[:, :KEEP].astype(jnp.int32)


def level_of(rng, dims, cuts, least, high):
    def one(dim, parts):
        heights = jax.random.uniform(jax.random.fold_in(jax.random.fold_in(rng, 6), dim), (parts,), jnp.float32, least / len(cuts), high / len(cuts))
        return jnp.repeat(jnp.exp(heights), dims[dim] // parts).reshape((-1,) + (1,) * (len(dims) - dim - 1))

    gain = one(*cuts[0])
    for cut in cuts[1:]:
        gain = gain * one(*cut)
    return gain


def gaussian(own_key, extent, width, most, split=(), held_as=jnp.bfloat16):
    drawn = jax.random.normal(own_key, extent, jnp.float32) * width
    if len(split) > 0:
        drawn = level_of(own_key, extent, split, -0.22, 0.18) * drawn
    return jnp.clip(drawn, min=-most, max=most).astype(held_as)


def setup_inputs(seed: int = 0) -> dict:
    key_list = jax.random.split(jax.random.key(seed), 20)
    visible = gaussian(key_list[0], (IMAGES, KEEP, DE), 1.0, 6.0, ((0, 32),))
    cotangent = gaussian(key_list[1], (IMAGES, PATCHES, DD), 1.0, 6.0, ((0, 32),))
    keep_index = draw_keep_index(jax.random.fold_in(key_list[19], 71), 0)
    positions = jnp.clip(jax.random.uniform(key_list[3], (PATCHES, DD), jnp.float32, -1.0, 1.0), -1.0, 1.0)
    enc_qkv = gaussian(key_list[4], (DE, 3 * DE), DE ** -0.5, 0.21875, ((0, 8), (1, 4)), jnp.float32)
    enc_out = gaussian(key_list[5], (DE, DE), (DE // 4) ** -0.5, 0.4375, ((0, 8), (1, 4)), jnp.float32)
    enc_up = gaussian(key_list[6], (DE, FE), DE ** -0.5, 0.21875, ((0, 8), (1, 4)), jnp.float32)
    enc_down = gaussian(key_list[7], (FE, DE), FE ** -0.5, 0.109375, ((0, 8), (1, 4)), jnp.float32)
    dec_embed = gaussian(key_list[8], (DE, DD), DE ** -0.5, 0.21875, ((0, 8), (1, 4)), jnp.float32)
    dec_qkv = gaussian(key_list[9], (DD, 3 * DD), DD ** -0.5, 0.25, ((0, 8), (1, 4)), jnp.float32)
    dec_out = gaussian(key_list[10], (DD, DD), (DD // 8) ** -0.5, 0.75, ((0, 8), (1, 4)), jnp.float32)
    dec_up = gaussian(key_list[11], (DD, FD), DD ** -0.5, 0.25, ((0, 8), (1, 4)), jnp.float32)
    dec_down = gaussian(key_list[12], (FD, DD), FD ** -0.5, 0.125, ((0, 8), (1, 4)), jnp.float32)
    enc_gains = jnp.clip(1.0 + 0.1 * jax.random.normal(key_list[13], (2, DE), jnp.float32), 0.5, 1.5)
    enc_biases = gaussian(key_list[14], (6, DE), 0.2, 1.2, ((1, 32),), jnp.float32)
    enc_up_bias = gaussian(key_list[15], (FE,), 0.2, 1.2, ((0, 32),), jnp.float32)
    dec_gains = jnp.clip(1.0 + 0.1 * jax.random.normal(key_list[16], (2, DD), jnp.float32), 0.5, 1.5)
    dec_biases = gaussian(key_list[17], (8, DD), 0.2, 1.2, ((1, 32),), jnp.float32)
    dec_up_bias = gaussian(key_list[18], (FD,), 0.2, 1.2, ((0, 32),), jnp.float32)
    return dict(visible=visible, cotangent=cotangent, keep_index=keep_index, positions=positions, enc_qkv=enc_qkv, enc_out=enc_out, enc_up=enc_up, enc_down=enc_down, dec_embed=dec_embed, dec_qkv=dec_qkv, dec_out=dec_out, dec_up=dec_up, dec_down=dec_down, enc_gains=enc_gains, enc_biases=enc_biases, enc_up_bias=enc_up_bias, dec_gains=dec_gains, dec_biases=dec_biases, dec_up_bias=dec_up_bias)


EPS = 1e-06
PRECISE = lax.Precision.HIGHEST

@jax.custom_vjp
def low(v):
    return lax.optimization_barrier(v.astype(jnp.bfloat16)).astype(jnp.float32)

@jax.custom_vjp
def low_back(v):
    return v

def low_keep(v):
    return (low(v), None)

def low_pass(kept, grad):
    return (grad,)

def back_keep(v):
    return (v, None)

def back_low(kept, grad):
    return (low(grad),)
low.defvjp(low_keep, low_pass)
low_back.defvjp(back_keep, back_low)

def layer_norm(values, norm_gain, norm_shift):
    average = lax.optimization_barrier(jnp.mean(values, axis=-1, keepdims=True))
    centred = values - average
    spread = lax.optimization_barrier(jnp.mean(centred * centred, axis=-1, keepdims=True))
    return centred * lax.rsqrt(spread + EPS) * norm_gain + norm_shift

def matmul_rows(left_rows, right_matrix):
    return jnp.einsum('bnc,cf->bnf', left_rows, right_matrix, precision=PRECISE)

def attention(inputs, norm_gain, norm_shift, w_qkv, bias_qkv, w_out, bias_out, head_count):
    normed = low(layer_norm(inputs, norm_gain, norm_shift))
    packed = low(low_back(matmul_rows(normed, w_qkv) + bias_qkv))
    batch_size, tokens, triple = packed.shape
    model_width = triple // 3
    head_size = model_width // head_count
    split_heads = packed.reshape(batch_size, tokens, 3, head_count, head_size)
    queries = split_heads[:, :, 0]
    keys_rows = split_heads[:, :, 1]
    values_rows = split_heads[:, :, 2]
    scores = low_back(jnp.einsum('bqhd,bkhd->bhqk', queries, keys_rows, precision=PRECISE) * head_size ** (-0.5))
    attention_probs = low(jax.nn.softmax(scores, axis=-1))
    mixed_heads = jnp.einsum('bhqk,bkhd->bqhd', attention_probs, values_rows, precision=PRECISE)
    mixed_heads = low(low_back(mixed_heads.reshape(batch_size, tokens, model_width)))
    return inputs + matmul_rows(mixed_heads, w_out) + bias_out

def feed_forward(inputs, norm_gain, norm_shift, w_up, bias_up, w_down, bias_down):
    normed = low(layer_norm(inputs, norm_gain, norm_shift))
    hidden = low_back(matmul_rows(normed, w_up) + bias_up)
    active = low(jax.nn.gelu(hidden, approximate=False))
    return inputs + matmul_rows(active, w_down) + bias_down

def forward_group(rounded, visible_rows, keep_rows, positions):
    enc_qkv, enc_out, enc_up, enc_down, dec_embed, dec_qkv, dec_out, dec_up, dec_down, enc_gains, enc_biases, enc_up_bias, dec_gains, dec_biases, dec_up_bias = rounded
    enc_zeros = jnp.zeros_like(enc_biases[1])
    dec_zeros = jnp.zeros_like(dec_biases[3])
    first_out = attention(visible_rows, enc_gains[0], enc_biases[0], enc_qkv, jnp.concatenate([enc_biases[1], enc_zeros, enc_biases[2]]), enc_out, enc_biases[3], HE)
    first_out = low(low_back(first_out))
    second_out = feed_forward(first_out, enc_gains[1], enc_biases[4], enc_up, enc_up_bias, enc_down, enc_biases[5])
    second_out = low(low_back(second_out))
    embedded = low_back(matmul_rows(second_out, dec_embed) + dec_biases[0])
    places = jnp.arange(PATCHES, dtype=jnp.int32)
    onehot = (keep_rows[:, None, :] == places[None, :, None]).astype(jnp.float32)
    covered = lax.optimization_barrier(jnp.sum(onehot, axis=2, keepdims=True))
    placed = jnp.einsum('bpj,bjc->bpc', onehot, embedded, precision=PRECISE) + (1.0 - covered) * dec_biases[1] + positions
    third_out = attention(placed, dec_gains[0], dec_biases[2], dec_qkv, jnp.concatenate([dec_biases[3], dec_zeros, dec_biases[4]]), dec_out, dec_biases[5], HD)
    third_out = low(low_back(third_out))
    return feed_forward(third_out, dec_gains[1], dec_biases[6], dec_up, dec_up_bias, dec_down, dec_biases[7])

def reference(visible, cotangent, keep_index, positions, enc_qkv, enc_out, enc_up, enc_down, dec_embed, dec_qkv, dec_out, dec_up, dec_down, enc_gains, enc_biases, enc_up_bias, dec_gains, dec_biases, dec_up_bias):
    masters = (enc_qkv, enc_out, enc_up, enc_down, dec_embed, dec_qkv, dec_out, dec_up, dec_down, enc_gains, enc_biases, enc_up_bias, dec_gains, dec_biases, dec_up_bias)
    image_count = visible.shape[0]
    group_size = min(16, image_count)
    group_count = image_count // group_size

    def whole(master_values, inputs):
        rounded = tuple((low(member) for member in master_values))

        def one_group(group_args):
            return forward_group(rounded, group_args[0], group_args[1], positions)
        grouped = (inputs.reshape((group_count, group_size) + inputs.shape[1:]), keep_index.reshape(group_count, group_size, keep_index.shape[1]))
        outputs = lax.map(jax.checkpoint(one_group), grouped)
        return outputs.reshape((image_count,) + outputs.shape[2:])
    block_out, pullback = jax.vjp(whole, masters, visible.astype(jnp.float32))
    grad_masters, input_grad = pullback(cotangent.astype(jnp.float32))
    return (block_out, input_grad, grad_masters[0], grad_masters[1], grad_masters[2], grad_masters[3], grad_masters[4], grad_masters[5], grad_masters[6], grad_masters[7], grad_masters[8], grad_masters[9], grad_masters[10], grad_masters[11], grad_masters[12], grad_masters[13], grad_masters[14])
```

```python
from functools import partial

import jax
import jax.numpy as jnp
from jax import lax
from jax.experimental import pallas as pl
from jax.experimental.pallas import tpu as pltpu
from jax.sharding import PartitionSpec as P

HE = 12
HD = 16
EPS = 1e-06
SEC = 4
ROWB = 8
BLOCKS = SEC * ROWB
ENC_ROWS = 64
DEC_ROWS = 208
BF = jnp.bfloat16
F32 = jnp.float32
VMEM_BYTES = 60 * 1024 * 1024


def dot(left, right):
    return jnp.dot(left, right, preferred_element_type=F32)


def dot_nt(left, right):
    return lax.dot_general(left, right, (((1,), (1,)), ((), ())), preferred_element_type=F32)


def dot_tn(left, right):
    return lax.dot_general(left, right, (((0,), (0,)), ((), ())), preferred_element_type=F32)


def norm_stats(values):
    centred = values - jnp.mean(values, axis=-1, keepdims=True)
    scale = lax.rsqrt(jnp.mean(centred * centred, axis=-1, keepdims=True) + EPS)
    return centred * scale, scale


def norm_back(grad, normed, scale, gain):
    inner = grad * gain
    mean_inner = jnp.mean(inner, axis=-1, keepdims=True)
    mean_cross = jnp.mean(inner * normed, axis=-1, keepdims=True)
    return scale * (inner - mean_inner - normed * mean_cross)


def column_sum(values):
    return jnp.sum(values, axis=0, keepdims=True)


def gelu_parts(values):
    share = 0.5 * (1.0 + lax.erf(values * (0.5**0.5)))
    return values * share, share


def gelu_slope(values, share):
    return share + values * (jnp.exp(-0.5 * values * values) * 0.3989422804014327)


def head_masks(width, size, dtype):
    lane = lax.broadcasted_iota(jnp.int32, (1, width), 1)
    return [
        jnp.where((lane >= h * size) & (lane < (h + 1) * size), 1.0, 0.0).astype(dtype)
        for h in range(width // size)
    ]


def stack_heads(window, size):
    return jnp.concatenate([window * m for m in head_masks(window.shape[1], size, window.dtype)], axis=0)


def unstack_heads(stacked, size):
    masks = head_masks(stacked.shape[1], size, stacked.dtype)
    rows = stacked.shape[0] // len(masks)
    total = stacked[:rows] * masks[0]
    for h in range(1, len(masks)):
        total = total + stacked[h * rows : (h + 1) * rows] * masks[h]
    return total


def softmax_rows(queries, keys, valid, size):
    scores = dot_nt(queries, keys) * size**-0.5
    lane = lax.broadcasted_iota(jnp.int32, (1, scores.shape[1]), 1)
    scores = jnp.where(lane < valid, scores, -1e30)
    powers = jnp.exp(scores - jnp.max(scores, axis=-1, keepdims=True))
    return powers / jnp.sum(powers, axis=-1, keepdims=True)


def attention_fwd(packed, width, size, valid, keep_probs):
    parts = []
    for w in range(width // 256):
        lanes = slice(256 * w, 256 * w + 256)
        queries = stack_heads(packed[:, lanes], size)
        keys = packed[:, width + 256 * w : width + 256 * w + 256]
        values = packed[:, 2 * width + 256 * w : 2 * width + 256 * w + 256]
        probs = softmax_rows(queries, keys, valid, size)
        if keep_probs is not None:
            keep_probs[w] = probs
        parts.append(unstack_heads(dot(probs.astype(BF), values), size))
    return jnp.concatenate(parts, axis=1).astype(BF)


def attention_bwd(packed, grad_mixed, width, size, valid, kept_probs):
    grad_q, grad_k, grad_v = [], [], []
    for w in range(width // 256):
        queries = stack_heads(packed[:, 256 * w : 256 * w + 256], size)
        keys = packed[:, width + 256 * w : width + 256 * w + 256]
        values = packed[:, 2 * width + 256 * w : 2 * width + 256 * w + 256]
        grads = stack_heads(grad_mixed[:, 256 * w : 256 * w + 256], size)
        probs = softmax_rows(queries, keys, valid, size) if kept_probs is None else kept_probs[w]
        grad_probs = dot_nt(grads, values)
        centre = jnp.sum(probs * grad_probs, axis=-1, keepdims=True)
        grad_scores = (probs * (grad_probs - centre)).astype(BF)
        grad_q.append(unstack_heads(dot(grad_scores, keys), size) * size**-0.5)
        grad_k.append(dot_tn(grad_scores, queries) * size**-0.5)
        grad_v.append(dot_tn(probs.astype(BF), grads))
    return jnp.concatenate(grad_q + grad_k + grad_v, axis=1).astype(BF)


def block_copies(pieces, table, rows, lanes, place, sem, store=False):
    copies = []
    number = 0
    for piece in pieces:
        for i in range(piece.shape[0]):
            outer = piece.at[i, pl.ds(*rows), pl.ds(*lanes)]
            inner = place(table[number])
            source, target = (inner, outer) if store else (outer, inner)
            copies.append(pltpu.make_async_copy(source, target, sem))
            number += 1
    for copy in copies:
        copy.start()
    return copies


def wait_all(copies):
    for copy in copies:
        copy.wait()


def rows_place(scratch, rows):
    def place(block):
        return scratch.at[block // ROWB, pl.ds(pl.multiple_of((block % ROWB) * rows, rows), rows), :]

    return place


def turned_place(scratch, rows, columns, first, count):
    def place(block):
        top = pl.multiple_of((block // ROWB) * rows + first, count)
        return scratch.at[pl.ds(top, count), pl.ds(pl.multiple_of((block % ROWB) * columns, columns), columns)]

    return place


def padded(values, rows):
    short = rows - values.shape[0]
    return jnp.concatenate([values, jnp.zeros((short, values.shape[1]), values.dtype)], axis=0)


def row_mask(rows, valid):
    return lax.broadcasted_iota(jnp.int32, (rows, 1), 0) < valid


def enc_att_fwd(count, table, x_ref, vec_ref, *refs):
    pieces, (h_ref, a_ref, k_ref, z_ref, w_ref, sem) = refs[:count], refs[count:]
    copies = block_copies(pieces, table, (0, 96), (0, 768), rows_place(w_ref, 96), sem)
    inputs = padded(x_ref[0].astype(F32), ENC_ROWS)
    normed, _ = norm_stats(inputs)
    low = (normed * vec_ref[0:1] + vec_ref[2:3]).astype(BF)
    a_ref[...] = low
    wait_all(copies)
    packed = jnp.concatenate([dot(low, w_ref[s, :, 0:640])[:, :576] for s in range(SEC)], axis=1)
    zero = jnp.zeros((1, 768), F32)
    packed = (packed + jnp.concatenate([vec_ref[3:4], zero, vec_ref[4:5]], axis=1)).astype(BF)
    k_ref[...] = packed
    mixed = attention_fwd(packed, 768, 64, 49, None)
    z_ref[...] = mixed
    result = jnp.concatenate([dot(mixed, w_ref[s, :, 512:768])[:, 64:] for s in range(SEC)], axis=1)
    h_ref[...] = (inputs + result + vec_ref[5:6]).astype(BF)


def enc_ffn_fwd(count, table, h_ref, vec_ref, upb_ref, *refs):
    ups, downs = refs[:count], refs[count : 2 * count]
    o_ref, a_ref, r_ref, u_ref, v_ref, sem_u, sem_v = refs[2 * count :]
    copies_u = block_copies(ups, table, (0, 96), (0, 768), rows_place(u_ref, 96), sem_u)
    copies_v = []
    for half in range(2):
        copies_v += block_copies(
            downs, table, (0, 96), (384 * half, 384), turned_place(v_ref, 192, 384, 96 * half, 96), sem_v
        )
    inputs = h_ref[...].astype(F32)
    normed, _ = norm_stats(inputs)
    low = (normed * vec_ref[1:2] + vec_ref[6:7]).astype(BF)
    a_ref[...] = low
    wait_all(copies_u)
    active = []
    for s in range(SEC):
        lanes = slice(768 * s, 768 * s + 768)
        hidden = dot(low, u_ref[s]) + upb_ref[:, lanes]
        r_ref[:, lanes] = hidden
        active.append(gelu_parts(hidden)[0].astype(BF))
    wait_all(copies_v)
    result = dot_nt(jnp.concatenate(active, axis=1), v_ref[...])
    o_ref[...] = (inputs + result + vec_ref[7:8]).astype(BF)


def placing(keep_ref):
    keep = jnp.concatenate([keep_ref[...], jnp.full((1, ENC_ROWS - 49), -1, jnp.int32)], axis=1)
    place = lax.broadcasted_iota(jnp.int32, (DEC_ROWS, ENC_ROWS), 0)
    return jnp.where(place == keep, 1.0, 0.0).astype(F32)


def dec_att_fwd(count, table, h_ref, keep_ref, pos_ref, vec_ref, *refs):
    embeds, pieces = refs[:count], refs[count : 2 * count]
    o_ref, u_ref, a_ref, k_ref, p_ref, z_ref, e_ref, w_ref, sem_e, sem_w = refs[2 * count :]
    copies_e = block_copies(embeds, table, (0, 96), (768, 128), rows_place(e_ref, 96), sem_e)
    copies_w = block_copies(pieces, table, (0, 64), (0, 512), rows_place(w_ref, 64), sem_w)
    onehot = placing(keep_ref)
    uncovered = 1.0 - jnp.sum(onehot, axis=1, keepdims=True)
    wait_all(copies_e)
    embedded = dot(h_ref[...], jnp.concatenate([e_ref[s] for s in range(SEC)], axis=1)) + vec_ref[2:3]
    placed = jnp.dot(onehot, embedded, precision=lax.Precision.HIGHEST, preferred_element_type=F32)
    placed = placed + uncovered * vec_ref[3:4] + padded(pos_ref[...], DEC_ROWS)
    u_ref[...] = placed
    normed, _ = norm_stats(placed)
    low = (normed * vec_ref[0:1] + vec_ref[4:5]).astype(BF)
    a_ref[...] = low
    wait_all(copies_w)
    packed = jnp.concatenate([dot(low, w_ref[s, :, 0:384]) for s in range(SEC)], axis=1)
    zero = jnp.zeros((1, 512), F32)
    packed = (packed + jnp.concatenate([vec_ref[5:6], zero, vec_ref[6:7]], axis=1)).astype(BF)
    k_ref[...] = packed
    mixed = attention_fwd(packed, 512, 32, 196, p_ref)
    z_ref[...] = mixed
    result = dot(mixed, jnp.concatenate([w_ref[s, :, 384:512] for s in range(SEC)], axis=1))
    o_ref[...] = (placed + result + vec_ref[7:8]).astype(BF)


def dec_ffn_both(count, outs, tables, h_ref, ct_ref, vec_ref, upb_ref, *refs):
    pieces = refs[:count]
    y_ref, dh_ref, gvec_ref, gupb_ref = refs[count : count + 4]
    grads = refs[count + 4 : count + 4 + outs]
    u_ref, v_ref, gu_ref, gv_ref, sem_u, sem_v, sem_o = refs[count + 4 + outs :]
    table, table_out = tables
    copies_u = block_copies(pieces, table, (0, 64), (512, 512), rows_place(u_ref, 64), sem_u)
    copies_v = []
    for half in range(2):
        copies_v += block_copies(
            pieces, table, (0, 64), (1024 + 256 * half, 256), turned_place(v_ref, 128, 256, 64 * half, 64), sem_v
        )
    inputs = h_ref[...].astype(F32)
    normed, scale = norm_stats(inputs)
    low = (normed * vec_ref[1:2] + vec_ref[8:9]).astype(BF)
    wait_all(copies_u)
    hidden, active = [], []
    for s in range(SEC):
        hidden.append(dot(low, u_ref[s]) + upb_ref[:, 512 * s : 512 * s + 512])
        active.append(gelu_parts(hidden[s])[0].astype(BF))
    active = jnp.concatenate(active, axis=1)
    wait_all(copies_v)
    result = inputs + dot_nt(active, v_ref[...]) + vec_ref[9:10]
    y_ref[0] = result[:196]
    grad_low = padded(ct_ref[0].astype(F32), DEC_ROWS).astype(BF)
    gv_ref[...] = dot_tn(grad_low, active).astype(BF)
    copies = []
    for half in range(2):
        copies += block_copies(
            grads, table_out, (0, 64), (512 + 256 * half, 256),
            turned_place(gv_ref, 128, 256, 64 * half, 64), sem_o, True,
        )
    grad_normed = jnp.zeros((DEC_ROWS, 512), F32)
    for s in range(SEC):
        lanes = slice(512 * s, 512 * s + 512)
        share = gelu_parts(hidden[s])[1]
        grad_hidden = (dot(grad_low, v_ref[:, lanes]) * gelu_slope(hidden[s], share)).astype(BF)
        gupb_ref[:, lanes] = column_sum(grad_hidden.astype(F32))
        gu_ref[s] = dot_tn(low, grad_hidden).astype(BF)
        grad_normed = grad_normed + dot_nt(grad_hidden, u_ref[s])
    copies += block_copies(grads, table_out, (0, 64), (0, 512), rows_place(gu_ref, 64), sem_o, True)
    grad_out = grad_low.astype(F32)
    gvec_ref[...] = jnp.concatenate(
        [column_sum(grad_normed * normed), column_sum(grad_normed), column_sum(grad_out)], axis=0
    )
    dh_ref[...] = (grad_out + norm_back(grad_normed, normed, scale, vec_ref[1:2])).astype(BF)
    wait_all(copies)


def dec_att_bwd(count, outs, tables, dh_ref, u_ref, a_ref, k_ref, p_ref, z_ref, h_ref, keep_ref, vec_ref, *refs):
    embeds, pieces = refs[:count], refs[count : 2 * count]
    dx_ref, gvec_ref = refs[2 * count : 2 * count + 2]
    grads = refs[2 * count + 2 : 2 * count + 2 + outs]
    grads_e = refs[2 * count + 2 + outs : 2 * count + 2 + 2 * outs]
    e_ref, w_ref, ge_ref, gw_ref, sem_e, sem_w, sem_o = refs[2 * count + 2 + 2 * outs :]
    table, table_out = tables
    copies_w = block_copies(pieces, table, (0, 64), (0, 512), rows_place(w_ref, 64), sem_w)
    copies_e = block_copies(embeds, table, (0, 96), (768, 128), rows_place(e_ref, 96), sem_e)
    grad = dh_ref[...]
    grad_out = grad.astype(F32)
    low, packed, mixed = a_ref[...], k_ref[...], z_ref[...]
    for s in range(SEC):
        gw_ref[s, :, 384:512] = dot_tn(mixed, grad[:, 128 * s : 128 * s + 128]).astype(BF)
    wait_all(copies_w)
    grad_mixed = dot_nt(grad, jnp.concatenate([w_ref[s, :, 384:512] for s in range(SEC)], axis=1)).astype(BF)
    grad_packed = attention_bwd(packed, grad_mixed, 512, 32, 196, p_ref)
    grad_normed = jnp.zeros((DEC_ROWS, 512), F32)
    for s in range(SEC):
        part = grad_packed[:, 384 * s : 384 * s + 384]
        gw_ref[s, :, 0:384] = dot_tn(low, part).astype(BF)
        grad_normed = grad_normed + dot_nt(part, w_ref[s, :, 0:384])
    copies = block_copies(grads, table_out, (0, 64), (0, 512), rows_place(gw_ref, 64), sem_o, True)
    normed, scale = norm_stats(u_ref[...])
    grad_placed = grad_out + norm_back(grad_normed, normed, scale, vec_ref[0:1])
    onehot = placing(keep_ref)
    uncovered = 1.0 - jnp.sum(onehot, axis=1, keepdims=True)
    grad_token = column_sum(uncovered * grad_placed)
    grad_embedded = lax.dot_general(
        onehot, grad_placed, (((0,), (0,)), ((), ())), precision=lax.Precision.HIGHEST, preferred_element_type=F32
    ).astype(BF)
    before = h_ref[...]
    for s in range(SEC):
        ge_ref[s] = dot_tn(before, grad_embedded[:, 128 * s : 128 * s + 128]).astype(BF)
    copies += block_copies(grads_e, table_out, (0, 96), (0, 128), rows_place(ge_ref, 96), sem_o, True)
    wait_all(copies_e)
    dx_ref[...] = dot_nt(grad_embedded, jnp.concatenate([e_ref[s] for s in range(SEC)], axis=1)).astype(BF)
    totals = column_sum(grad_packed.astype(F32))
    gvec_ref[...] = jnp.concatenate(
        [
            column_sum(grad_normed * normed),
            column_sum(grad_embedded.astype(F32)),
            grad_token,
            column_sum(grad_normed),
            totals[:, :512],
            totals[:, 1024:],
            column_sum(grad_out),
        ],
        axis=0,
    )
    wait_all(copies)


def enc_ffn_bwd(count, outs, tables, dh_ref, h_ref, a_ref, r_ref, vec_ref, *refs):
    ups, downs = refs[:count], refs[count : 2 * count]
    dx_ref, gvec_ref, gupb_ref = refs[2 * count : 2 * count + 3]
    grads_u = refs[2 * count + 3 : 2 * count + 3 + outs]
    grads_v = refs[2 * count + 3 + outs : 2 * count + 3 + 2 * outs]
    u_ref, v_ref, gu_ref, gv_ref, sem_u, sem_v, sem_o = refs[2 * count + 3 + 2 * outs :]
    table, table_out = tables
    copies_v = []
    for half in range(2):
        copies_v += block_copies(
            downs, table, (0, 96), (384 * half, 384), turned_place(v_ref, 192, 384, 96 * half, 96), sem_v
        )
    copies_u = block_copies(ups, table, (0, 96), (0, 768), rows_place(u_ref, 96), sem_u)
    grad = dh_ref[...]
    grad_out = grad.astype(F32)
    low = a_ref[...]
    wait_all(copies_v)
    wait_all(copies_u)
    grad_normed = jnp.zeros((ENC_ROWS, 768), F32)
    for s in range(SEC):
        lanes = slice(768 * s, 768 * s + 768)
        hidden = r_ref[:, lanes]
        active, share = gelu_parts(hidden)
        gv_ref[:, lanes] = dot_tn(grad, active.astype(BF)).astype(BF)
        grad_hidden = (dot(grad, v_ref[:, lanes]) * gelu_slope(hidden, share)).astype(BF)
        gupb_ref[:, lanes] = column_sum(grad_hidden.astype(F32))
        gu_ref[s] = dot_tn(low, grad_hidden).astype(BF)
        grad_normed = grad_normed + dot_nt(grad_hidden, u_ref[s])
    copies = block_copies(grads_u, table_out, (0, 96), (0, 768), rows_place(gu_ref, 96), sem_o, True)
    for half in range(2):
        copies += block_copies(
            grads_v, table_out, (0, 96), (384 * half, 384),
            turned_place(gv_ref, 192, 384, 96 * half, 96), sem_o, True,
        )
    normed, scale = norm_stats(h_ref[...].astype(F32))
    gvec_ref[...] = jnp.concatenate(
        [column_sum(grad_normed * normed), column_sum(grad_normed), column_sum(grad_out)], axis=0
    )
    dx_ref[...] = (grad_out + norm_back(grad_normed, normed, scale, vec_ref[1:2])).astype(BF)
    wait_all(copies)


def enc_att_bwd(count, outs, tables, dh_ref, x_ref, a_ref, k_ref, z_ref, vec_ref, *refs):
    pieces = refs[:count]
    dx_ref, gvec_ref = refs[count : count + 2]
    grads = refs[count + 2 : count + 2 + outs]
    w_ref, g_ref, sem_w, sem_o = refs[count + 2 + outs :]
    table, table_out = tables
    copies_w = block_copies(pieces, table, (0, 96), (0, 768), rows_place(w_ref, 96), sem_w)
    grad = dh_ref[...]
    grad_out = grad.astype(F32)
    low, packed, mixed = a_ref[...], k_ref[...], z_ref[...]
    wait_all(copies_w)
    gap = jnp.zeros((ENC_ROWS, 64), BF)
    parts = [grad[:, 192 * s : 192 * s + 192] for s in range(SEC)]
    grad_mixed = jnp.zeros((ENC_ROWS, 768), F32)
    for s in range(SEC):
        grad_mixed = grad_mixed + dot_nt(jnp.concatenate([gap, parts[s]], axis=1), w_ref[s, :, 512:768])
    grad_packed = attention_bwd(packed, grad_mixed.astype(BF), 768, 64, 49, None)
    grad_normed = jnp.zeros((ENC_ROWS, 768), F32)
    both = jnp.concatenate([low, mixed], axis=0)
    for s in range(SEC):
        part = grad_packed[:, 576 * s : 576 * s + 576]
        grad_normed = grad_normed + dot_nt(jnp.concatenate([part, gap], axis=1), w_ref[s, :, 0:640])
        right = jnp.concatenate(
            [
                jnp.concatenate([part, jnp.zeros((ENC_ROWS, 192), BF)], axis=1),
                jnp.concatenate([jnp.zeros((ENC_ROWS, 576), BF), parts[s]], axis=1),
            ],
            axis=0,
        )
        g_ref[s] = dot_tn(both, right).astype(BF)
    copies = block_copies(grads, table_out, (0, 96), (0, 768), rows_place(g_ref, 96), sem_o, True)
    normed, scale = norm_stats(padded(x_ref[0].astype(F32), ENC_ROWS))
    grad_in = grad_out + norm_back(grad_normed, normed, scale, vec_ref[0:1])
    dx_ref[0] = grad_in[:49]
    totals = column_sum(grad_packed.astype(F32))
    gvec_ref[...] = jnp.concatenate(
        [
            column_sum(grad_normed * normed),
            column_sum(grad_normed),
            totals[:, :768],
            totals[:, 1536:],
            column_sum(grad_out),
        ],
        axis=0,
    )
    wait_all(copies)


def call(body, outs, scratch, *operands, memory):
    spaces = {"v": pltpu.VMEM, "s": pltpu.SMEM, "h": pl.ANY}
    return pl.pallas_call(
        body,
        out_shape=[jax.ShapeDtypeStruct(shape, dtype) for shape, dtype, _ in outs],
        in_specs=[pl.BlockSpec(memory_space=spaces[m]) for m in memory],
        out_specs=[pl.BlockSpec(memory_space=spaces[m]) for _, _, m in outs],
        scratch_shapes=scratch,
        compiler_params=pltpu.CompilerParams(vmem_limit_bytes=VMEM_BYTES),
    )(*operands)


def with_tables(body, count, outs):
    def kernel(table, table_out, *refs):
        body(count, outs, (table, table_out), *refs)

    return kernel


def fold_rows(matrix):
    half = matrix.shape[-2] // 2
    return jnp.concatenate([matrix[..., :half, :], matrix[..., half:, :]], axis=-1)


def unfold_rows(matrix):
    half = matrix.shape[-1] // 2
    return jnp.concatenate([matrix[..., :half], matrix[..., half:]], axis=-2)


def turn(matrix):
    return jnp.swapaxes(matrix, -1, -2)


def pack_weights(qkv_e, out_e, up_e, down_e, embed, qkv_d, out_d, up_d, down_d):
    return (
        jnp.concatenate([qkv_e, out_e, embed], axis=-1),
        up_e,
        fold_rows(turn(down_e)),
        jnp.concatenate([qkv_d, out_d, up_d, fold_rows(turn(down_d))], axis=-1),
    )


def unpack_grads(ffn_d, att_d, embed, up_e, down_e, att_e):
    return (
        att_e[..., :576],
        att_e[..., 576:],
        up_e,
        turn(unfold_rows(down_e)),
        embed,
        att_d[..., :384],
        att_d[..., 384:],
        ffn_d[..., :512],
        turn(unfold_rows(ffn_d[..., 512:])),
    )


def join_vectors(enc, dec, up_e, up_d):
    return jnp.concatenate([enc.reshape(1, -1), dec.reshape(1, -1), up_e.reshape(1, -1), up_d.reshape(1, -1)], axis=1)


def spread_vectors(rows):
    devices = rows.shape[0]
    a, b, c, d = 8 * 768 // devices, 10 * 512 // devices, 3072 // devices, 2048 // devices
    enc = rows[:, :a].reshape(devices, 8, -1).transpose(1, 0, 2).reshape(8, 768)
    dec = rows[:, a : a + b].reshape(devices, 10, -1).transpose(1, 0, 2).reshape(10, 512)
    return enc, dec, rows[:, a + b : a + b + c].reshape(1, 3072), rows[:, a + b + c :].reshape(1, 2048)


def collect_vectors(enc, dec, up_e, up_d, devices):
    enc = enc.reshape(8, devices, -1).transpose(1, 0, 2).reshape(devices, -1)
    dec = dec.reshape(10, devices, -1).transpose(1, 0, 2).reshape(devices, -1)
    return jnp.concatenate([enc, dec, up_e.reshape(devices, -1), up_d.reshape(devices, -1)], axis=1)


def split_vectors(row, devices):
    a, b, c = 8 * 768 // devices, 10 * 512 // devices, 3072 // devices
    enc = row[:, :a].reshape(8, -1)
    dec = row[:, a : a + b].reshape(10, -1)
    return enc[:2], enc[2:], row[0, a + b : a + b + c], dec[:2], dec[2:], row[0, a + b + c :]

def exchange(value, flip):
    pairs = [(device, device ^ flip(device)) for device in range(BLOCKS)]
    return lax.ppermute(value, ("section", "dp"), pairs)


def across_core(device):
    return 1


def across_near(device):
    return 2


def across_far(device):
    return 4


def across_first(device):
    return 16 if device & 1 else 8


def across_second(device):
    return 8 if device & 1 else 16


STEPS = (across_near, across_far, across_first, across_second)


def block_at(device, core, relative):
    here = (device & 30) | core
    first = jnp.where(core == 1, 16, 8)
    second = jnp.where(core == 1, 8, 16)
    flips = 2 * (relative & 1) + 4 * ((relative >> 1) & 1) + first * ((relative >> 2) & 1) + second * ((relative >> 3) & 1)
    return here ^ flips


def gather_pieces(member):
    held = member[None]
    for step in STEPS[:3]:
        held = jnp.concatenate([held, exchange(held, step)], axis=0)
    rest = exchange(held, STEPS[3])
    return [held, rest, exchange(held, across_core), exchange(rest, across_core)]


def sum_pieces(sent, kept):
    total = kept.astype(F32) + exchange(sent, across_core).astype(F32)
    for step in STEPS[::-1]:
        half = total.shape[0] // 2
        arrived = exchange(total[:half].astype(BF), step)
        total = total[half:] + arrived.astype(F32)
    return total[0]


def shards(visible, cotangent, keep_index, positions, *parameters):
    both = ("section", "dp")
    devices = lax.axis_size("section") * lax.axis_size("dp")
    fast = lax.axis_size("dp") == ROWB
    lowered = [member.astype(BF) for member in parameters]
    matrices, (enc_g, enc_b, enc_u, dec_g, dec_b, dec_u) = lowered[:9], lowered[9:]
    vector_row = join_vectors(
        jnp.concatenate([enc_g, enc_b]), jnp.concatenate([dec_g, dec_b]), enc_u, dec_u
    )
    if fast:
        packed = list(pack_weights(*matrices))
        extra = jnp.zeros((16, 896), BF).at[:1, : vector_row.shape[1]].set(vector_row)
        packed[0] = jnp.concatenate([packed[0], extra], axis=0)
        device = lax.axis_index(both)
        core = device & 1
        order = jnp.arange(16, dtype=jnp.int32)
        table = jnp.concatenate([block_at(device, core, order), block_at(device, 1 - core, order)])
        table_out = jnp.concatenate([block_at(device, 1 - core, 15 - order), block_at(device, core, 15 - order)])
        att_e, up_e, down_e, dec = [gather_pieces(member) for member in packed]
        arrived = jnp.concatenate([piece[:, 96, : vector_row.shape[1]] for piece in att_e], axis=0)
        canonical = jnp.arange(BLOCKS, dtype=jnp.int32)[:, None]
        vector_rows = dot((table[None, :] == canonical).astype(BF), arrived)
    else:
        full = []
        for member in matrices:
            member = lax.all_gather(member, "dp", axis=0, tiled=True)
            member = lax.all_gather(member, "section", axis=0, tiled=False)
            full.append(member.reshape(BLOCKS, member.shape[1] // ROWB, member.shape[2]))
        whole = pack_weights(*full)
        vector_rows = lax.all_gather(vector_row, both, axis=0, tiled=True)
        table = jnp.arange(BLOCKS, dtype=jnp.int32)
        table_out = table
        att_e, up_e, down_e, dec = ([member] for member in whole)
    enc_vec, dec_vec, enc_upb, dec_upb = spread_vectors(vector_rows.astype(F32))
    n = len(att_e)
    outs = 2 if fast else 1
    dma = pltpu.SemaphoreType.DMA
    enc_shape, dec_shape = (ENC_ROWS, 768), (DEC_ROWS, 512)

    def grad_blocks(rows, columns):
        return [((BLOCKS // outs, rows, columns), BF, "h")] * outs

    h1, a1, k1, z1 = call(
        partial(enc_att_fwd, n),
        [(enc_shape, BF, "v"), (enc_shape, BF, "v"), ((ENC_ROWS, 2304), BF, "v"), (enc_shape, BF, "v")],
        [pltpu.VMEM((SEC, 768, 768), BF), dma],
        table, visible, enc_vec, *att_e,
        memory="svv" + "h" * n,
    )
    h2, a2, r2 = call(
        partial(enc_ffn_fwd, n),
        [(enc_shape, BF, "v"), (enc_shape, BF, "v"), ((ENC_ROWS, 3072), F32, "v")],
        [pltpu.VMEM((SEC, 768, 768), BF), pltpu.VMEM((768, 3072), BF), dma, dma],
        table, h1, enc_vec, enc_upb, *up_e, *down_e,
        memory="svvv" + "h" * (2 * n),
    )
    h3, u3, a3, k3, p3, z3 = call(
        partial(dec_att_fwd, n),
        [
            (dec_shape, BF, "v"), (dec_shape, F32, "v"), (dec_shape, BF, "v"), ((DEC_ROWS, 1536), BF, "v"),
            ((2, 8 * DEC_ROWS, DEC_ROWS), F32, "v"), (dec_shape, BF, "v"),
        ],
        [pltpu.VMEM((SEC, 768, 128), BF), pltpu.VMEM((SEC, 512, 512), BF), dma, dma],
        table, h2, keep_index, positions, dec_vec, *att_e, *dec,
        memory="svvvv" + "h" * (2 * n),
    )
    block_out, dh3, gv_ffn_d, gupb_d, *g_ffn_d = call(
        with_tables(dec_ffn_both, n, outs),
        [((1, 196, 512), F32, "v"), (dec_shape, BF, "v"), ((3, 512), F32, "v"), ((1, 2048), F32, "v")]
        + grad_blocks(64, 1024),
        [pltpu.VMEM((SEC, 512, 512), BF), pltpu.VMEM((512, 2048), BF)] * 2 + [dma] * 3,
        table, table_out, h3, cotangent, dec_vec, dec_upb, *dec,
        memory="ssvvvv" + "h" * n,
    )
    dh2, gv_att_d, *g_att_d = call(
        with_tables(dec_att_bwd, n, outs),
        [(enc_shape, BF, "v"), ((7, 512), F32, "v")]
        + grad_blocks(64, 512) + grad_blocks(96, 128),
        [pltpu.VMEM((SEC, 768, 128), BF), pltpu.VMEM((SEC, 512, 512), BF)] * 2 + [dma] * 3,
        table, table_out, dh3, u3, a3, k3, p3, z3, h2, keep_index, dec_vec, *att_e, *dec,
        memory="ss" + "v" * 9 + "h" * (2 * n),
    )
    dh1, gv_ffn_e, gupb_e, *g_ffn_e = call(
        with_tables(enc_ffn_bwd, n, outs),
        [(enc_shape, BF, "v"), ((3, 768), F32, "v"), ((1, 3072), F32, "v")]
        + grad_blocks(96, 768) * 2,
        [pltpu.VMEM((SEC, 768, 768), BF), pltpu.VMEM((768, 3072), BF)] * 2 + [dma] * 3,
        table, table_out, dh2, h1, a2, r2, enc_vec, *up_e, *down_e,
        memory="ss" + "v" * 5 + "h" * (2 * n),
    )
    input_grad, gv_att_e, *g_att_e = call(
        with_tables(enc_att_bwd, n, outs),
        [((1, 49, 768), F32, "v"), ((5, 768), F32, "v")] + grad_blocks(112 if fast else 96, 768),
        [pltpu.VMEM((SEC, 768, 768), BF)] * 2 + [dma] * 2,
        table, table_out, dh1, visible, a1, k1, z1, enc_vec, *att_e,
        memory="ss" + "v" * 6 + "h" * n,
    )
    grad_enc = jnp.concatenate([gv_att_e[:1], gv_ffn_e[:1], gv_att_e[1:], gv_ffn_e[1:]])
    grad_dec = jnp.concatenate([gv_att_d[:1], gv_ffn_d[:1], gv_att_d[1:], gv_ffn_d[1:]])
    rows = collect_vectors(grad_enc, grad_dec, gupb_e, gupb_d, devices)
    blocks = [g_ffn_d, g_att_d[:outs], g_att_d[outs:], g_ffn_e[:outs], g_ffn_e[outs:], g_att_e]
    if fast:
        placed = jnp.dot((table_out[:, None] == canonical.T).astype(BF), rows.astype(BF))
        wide = rows.shape[1]
        blocks[5] = [
            member.at[:, 96, :wide].set(placed[16 * i : 16 * i + 16].astype(BF)) for i, member in enumerate(g_att_e)
        ]
        sums = [sum_pieces(*member) for member in blocks]
        row = sums[5][96:97, :wide]
        sums[5] = sums[5][:96]
        matrix_outs = unpack_grads(*sums)
    else:
        matrix_outs = []
        for member in unpack_grads(*(member[0] for member in blocks)):
            member = member.reshape(SEC, ROWB * member.shape[1], member.shape[2])
            member = lax.psum_scatter(member, "section", scatter_dimension=0, tiled=False)
            matrix_outs.append(lax.psum_scatter(member, "dp", scatter_dimension=0, tiled=True).astype(F32))
        row = lax.psum_scatter(rows, both, scatter_dimension=0, tiled=True)
    return (block_out, input_grad, *matrix_outs, *split_vectors(row, devices))


def solution(mesh):
    matrix, wide, line = P("dp", "section"), P(None, ("section", "dp")), P(("section", "dp"))
    image = P(("section", "dp"), None, None)
    vectors = (wide, wide, line, wide, wide, line)
    return jax.shard_map(
        shards,
        mesh=mesh,
        in_specs=(image, image, P(("section", "dp"), None), P()) + (matrix,) * 9 + vectors,
        out_specs=(image, image) + (matrix,) * 9 + vectors,
        check_vma=False,
    )
```

```python
from functools import partial

import jax
import jax.numpy as jnp
from jax import lax
from jax.experimental import pallas as pl
from jax.experimental.pallas import tpu as pltpu
from jax.sharding import PartitionSpec as P

HE = 12
HD = 16
EPS = 1e-06
SEC = 4
ROWB = 8
BLOCKS = SEC * ROWB
ENC_ROWS = 64
DEC_ROWS = 208
BF = jnp.bfloat16
F32 = jnp.float32
IN_PATH, IN_PLAIN, OUT_PATH, OUT_Z, SECTION = 0, BLOCKS, 2 * BLOCKS, 3 * BLOCKS, 3 * BLOCKS + ROWB
VMEM_BYTES = 60 * 1024 * 1024


def dot(left, right):
    return jnp.dot(left, right, preferred_element_type=F32)


def dot_nt(left, right):
    return lax.dot_general(left, right, (((1,), (1,)), ((), ())), preferred_element_type=F32)


def dot_tn(left, right):
    return lax.dot_general(left, right, (((0,), (0,)), ((), ())), preferred_element_type=F32)


def norm_stats(values):
    centred = values - jnp.mean(values, axis=-1, keepdims=True)
    scale = lax.rsqrt(jnp.mean(centred * centred, axis=-1, keepdims=True) + EPS)
    return centred * scale, scale


def norm_back(grad, normed, scale, gain):
    inner = grad * gain
    mean_inner = jnp.mean(inner, axis=-1, keepdims=True)
    mean_cross = jnp.mean(inner * normed, axis=-1, keepdims=True)
    return scale * (inner - mean_inner - normed * mean_cross)


def column_sum(values):
    return jnp.sum(values, axis=0, keepdims=True)


def gelu_parts(values):
    share = 0.5 * (1.0 + lax.erf(values * (0.5**0.5)))
    return values * share, share


def gelu_slope(values, share):
    return share + values * (jnp.exp(-0.5 * values * values) * 0.3989422804014327)


def head_masks(width, size, dtype):
    lane = lax.broadcasted_iota(jnp.int32, (1, width), 1)
    return [
        jnp.where((lane >= h * size) & (lane < (h + 1) * size), 1.0, 0.0).astype(dtype)
        for h in range(width // size)
    ]


def stack_heads(window, size):
    return jnp.concatenate([window * m for m in head_masks(window.shape[1], size, window.dtype)], axis=0)


def unstack_heads(stacked, size):
    masks = head_masks(stacked.shape[1], size, stacked.dtype)
    rows = stacked.shape[0] // len(masks)
    total = stacked[:rows] * masks[0]
    for h in range(1, len(masks)):
        total = total + stacked[h * rows : (h + 1) * rows] * masks[h]
    return total


def softmax_rows(queries, keys, valid, size):
    scores = dot_nt(queries, keys) * size**-0.5
    lane = lax.broadcasted_iota(jnp.int32, (1, scores.shape[1]), 1)
    scores = jnp.where(lane < valid, scores, -1e30)
    powers = jnp.exp(scores - jnp.max(scores, axis=-1, keepdims=True))
    return powers / jnp.sum(powers, axis=-1, keepdims=True)


def attention_fwd(packed, width, size, valid, keep_probs):
    parts = []
    for w in range(width // 256):
        lanes = slice(256 * w, 256 * w + 256)
        queries = stack_heads(packed[:, lanes], size)
        keys = packed[:, width + 256 * w : width + 256 * w + 256]
        values = packed[:, 2 * width + 256 * w : 2 * width + 256 * w + 256]
        probs = softmax_rows(queries, keys, valid, size)
        if keep_probs is not None:
            keep_probs[w] = probs
        parts.append(unstack_heads(dot(probs.astype(BF), values), size))
    return jnp.concatenate(parts, axis=1).astype(BF)


def attention_bwd(packed, grad_mixed, width, size, valid, kept_probs):
    grad_q, grad_k, grad_v = [], [], []
    for w in range(width // 256):
        queries = stack_heads(packed[:, 256 * w : 256 * w + 256], size)
        keys = packed[:, width + 256 * w : width + 256 * w + 256]
        values = packed[:, 2 * width + 256 * w : 2 * width + 256 * w + 256]
        grads = stack_heads(grad_mixed[:, 256 * w : 256 * w + 256], size)
        probs = softmax_rows(queries, keys, valid, size) if kept_probs is None else kept_probs[w]
        grad_probs = dot_nt(grads, values)
        centre = jnp.sum(probs * grad_probs, axis=-1, keepdims=True)
        grad_scores = (probs * (grad_probs - centre)).astype(BF)
        grad_q.append(unstack_heads(dot(grad_scores, keys), size) * size**-0.5)
        grad_k.append(dot_tn(grad_scores, queries) * size**-0.5)
        grad_v.append(dot_tn(probs.astype(BF), grads))
    return jnp.concatenate(grad_q + grad_k + grad_v, axis=1).astype(BF)


def block_copies(pieces, table, first, rows, lanes, place, sem, store=False):
    copies = []
    number = first
    for piece in pieces:
        for i in range(piece.shape[0]):
            outer = piece.at[i, pl.ds(*rows), pl.ds(*lanes)]
            inner = place(table[number])
            source, target = (inner, outer) if store else (outer, inner)
            copies.append(pltpu.make_async_copy(source, target, sem))
            number += 1
    for copy in copies:
        copy.start()
    return copies


def wait_all(copies):
    for copy in copies:
        copy.wait()


def rows_place(scratch, rows):
    def place(block):
        return scratch.at[block // ROWB, pl.ds(pl.multiple_of((block % ROWB) * rows, rows), rows), :]

    return place


def turned_place(scratch, rows, columns, first, count):
    def place(block):
        top = pl.multiple_of((block // ROWB) * rows + first, count)
        return scratch.at[pl.ds(top, count), pl.ds(pl.multiple_of((block % ROWB) * columns, columns), columns)]

    return place


def part_place(scratch, first, count):
    def place(block):
        top = pl.multiple_of((block % ROWB) * 96 + first, 32)
        return scratch.at[block // ROWB, pl.ds(top, count), :]

    return place


def take(refs, sizes):
    groups = []
    for count, _ in sizes:
        groups.append(refs[:count])
        refs = refs[count:]
    return groups, refs


def padded(values, rows):
    short = rows - values.shape[0]
    return jnp.concatenate([values, jnp.zeros((short, values.shape[1]), values.dtype)], axis=0)


def row_mask(rows, valid):
    return lax.broadcasted_iota(jnp.int32, (rows, 1), 0) < valid


def unpack_vectors(rows_ref, enc_ref, upe_ref, dec_ref, upd_ref):
    def joined(first, count, width):
        parts = [rows_ref[b, :count, first : first + width].astype(F32) for b in range(BLOCKS)]
        return jnp.concatenate(parts, axis=1)

    enc_ref[...] = joined(0, 8, 24)
    upe_ref[...] = joined(128, 1, 96)
    upd_ref[...] = joined(128, 2, 64)[1:]
    dec_ref[...] = jnp.concatenate([joined(256, 8, 16), joined(384, 2, 16)], axis=0)


def enc_att_fwd(inn, table, x_ref, *refs):
    (pieces,), (h_ref, a_ref, k_ref, z_ref, *rest) = take(refs, inn)
    if len(rest) == 3:
        vec_ref, w_ref, sem = rest
        copies = block_copies(pieces, table, inn[0][1], (0, 96), (0, 768), rows_place(w_ref, 96), sem)
    else:
        vec_ref, upe_ref, dec_ref, upd_ref, w_ref, rows_ref, sem, sem_v = rest
        first = block_copies(pieces, table, inn[0][1], (96, 16), (0, 512), lambda block: rows_ref.at[block], sem_v)
        copies = block_copies(pieces, table, inn[0][1], (0, 96), (0, 768), rows_place(w_ref, 96), sem)
        wait_all(first)
        unpack_vectors(rows_ref, vec_ref, upe_ref, dec_ref, upd_ref)
    inputs = padded(x_ref[0].astype(F32), ENC_ROWS)
    normed, _ = norm_stats(inputs)
    low = (normed * vec_ref[0:1] + vec_ref[2:3]).astype(BF)
    a_ref[...] = low
    wait_all(copies)
    packed = jnp.concatenate([dot(low, w_ref[s, :, 0:640])[:, :576] for s in range(SEC)], axis=1)
    zero = jnp.zeros((1, 768), F32)
    packed = (packed + jnp.concatenate([vec_ref[3:4], zero, vec_ref[4:5]], axis=1)).astype(BF)
    k_ref[...] = packed
    mixed = attention_fwd(packed, 768, 64, 49, None)
    z_ref[...] = mixed
    result = jnp.concatenate([dot(mixed, w_ref[s, :, 512:768])[:, 64:] for s in range(SEC)], axis=1)
    h_ref[...] = (inputs + result + vec_ref[5:6]).astype(BF)


def enc_ffn_fwd(inn, table, h_ref, vec_ref, upb_ref, *refs):
    (ups, downs), (o_ref, a_ref, r_ref, u_ref, v_ref, sem_u, sem_v) = take(refs, inn)
    copies_u = block_copies(ups, table, inn[0][1], (0, 96), (0, 768), rows_place(u_ref, 96), sem_u)
    copies_v = []
    for half in range(2):
        copies_v += block_copies(
            downs, table, inn[1][1], (0, 96), (384 * half, 384), turned_place(v_ref, 192, 384, 96 * half, 96), sem_v
        )
    inputs = h_ref[...].astype(F32)
    normed, _ = norm_stats(inputs)
    low = (normed * vec_ref[1:2] + vec_ref[6:7]).astype(BF)
    a_ref[...] = low
    wait_all(copies_u)
    active = []
    for s in range(SEC):
        lanes = slice(768 * s, 768 * s + 768)
        hidden = dot(low, u_ref[s]) + upb_ref[:, lanes]
        r_ref[:, lanes] = hidden
        active.append(gelu_parts(hidden)[0].astype(BF))
    wait_all(copies_v)
    result = dot_nt(jnp.concatenate(active, axis=1), v_ref[...])
    o_ref[...] = (inputs + result + vec_ref[7:8]).astype(BF)


def placing(keep_ref):
    keep = jnp.concatenate([keep_ref[...], jnp.full((1, ENC_ROWS - 49), -1, jnp.int32)], axis=1)
    place = lax.broadcasted_iota(jnp.int32, (DEC_ROWS, ENC_ROWS), 0)
    return jnp.where(place == keep, 1.0, 0.0).astype(F32)


def dec_both(inn, outs, table, h_ref, keep_ref, pos_ref, ct_ref, vec_ref, upb_ref, *refs):
    (pieces,), (y_ref, dx_ref, gvec_ref, gupb_ref, *rest) = take(refs, inn)
    (grads,), rest = take(rest, (outs,))
    e_ref, w_ref, u_ref, v_ref, ge_ref, gw_ref, gu_ref, gv_ref, p_ref, sem_e, sem_w, sem_u, sem_v, sem_o = rest
    start = inn[0][1]
    copies_e = block_copies(pieces, table, start, (0, 64), (1536, 128), part_place(e_ref, 0, 64), sem_e)
    copies_e += block_copies(pieces, table, start, (0, 32), (1664, 128), part_place(e_ref, 64, 32), sem_e)
    copies_w = block_copies(pieces, table, start, (0, 64), (0, 512), rows_place(w_ref, 64), sem_w)
    copies_u = block_copies(pieces, table, start, (0, 64), (512, 512), rows_place(u_ref, 64), sem_u)
    copies_v = []
    for half in range(2):
        copies_v += block_copies(
            pieces, table, start, (0, 64), (1024 + 256 * half, 256), turned_place(v_ref, 128, 256, 64 * half, 64), sem_v
        )
    copies = []

    def give(lanes, place, rows=64):
        copies.extend(block_copies(grads, table, outs[1], (0, rows), lanes, place, sem_o, True))

    before = h_ref[...]
    onehot = placing(keep_ref)
    uncovered = 1.0 - jnp.sum(onehot, axis=1, keepdims=True)
    wait_all(copies_e)
    embedded = dot(before, jnp.concatenate([e_ref[s] for s in range(SEC)], axis=1)) + vec_ref[2:3]
    placed = jnp.dot(onehot, embedded, precision=lax.Precision.HIGHEST, preferred_element_type=F32)
    placed = placed + uncovered * vec_ref[3:4] + padded(pos_ref[...], DEC_ROWS)
    normed_a, scale_a = norm_stats(placed)
    low_a = (normed_a * vec_ref[0:1] + vec_ref[4:5]).astype(BF)
    wait_all(copies_w)
    packed = jnp.concatenate([dot(low_a, w_ref[s, :, 0:384]) for s in range(SEC)], axis=1)
    zero = jnp.zeros((1, 512), F32)
    packed = (packed + jnp.concatenate([vec_ref[5:6], zero, vec_ref[6:7]], axis=1)).astype(BF)
    mixed = attention_fwd(packed, 512, 32, 196, p_ref)
    w_out = jnp.concatenate([w_ref[s, :, 384:512] for s in range(SEC)], axis=1)
    inputs = (placed + dot(mixed, w_out) + vec_ref[7:8]).astype(BF).astype(F32)

    normed, scale = norm_stats(inputs)
    low = (normed * vec_ref[1:2] + vec_ref[8:9]).astype(BF)
    wait_all(copies_u)
    hidden, active = [], []
    for s in range(SEC):
        hidden.append(dot(low, u_ref[s]) + upb_ref[:, 512 * s : 512 * s + 512])
        active.append(gelu_parts(hidden[s])[0].astype(BF))
    active = jnp.concatenate(active, axis=1)
    wait_all(copies_v)
    result = inputs + dot_nt(active, v_ref[...]) + vec_ref[9:10]
    y_ref[0] = result[:196]

    grad_low = padded(ct_ref[0].astype(F32), DEC_ROWS).astype(BF)
    gv_ref[...] = dot_tn(grad_low, active).astype(BF)
    for half in range(2):
        give((512 + 256 * half, 256), turned_place(gv_ref, 128, 256, 64 * half, 64))
    grad_normed = jnp.zeros((DEC_ROWS, 512), F32)
    for s in range(SEC):
        lanes = slice(512 * s, 512 * s + 512)
        share = gelu_parts(hidden[s])[1]
        grad_hidden = (dot(grad_low, v_ref[:, lanes]) * gelu_slope(hidden[s], share)).astype(BF)
        gupb_ref[:, lanes] = column_sum(grad_hidden.astype(F32))
        gu_ref[s] = dot_tn(low, grad_hidden).astype(BF)
        grad_normed = grad_normed + dot_nt(grad_hidden, u_ref[s])
    give((0, 512), rows_place(gu_ref, 64))
    grad_out = grad_low.astype(F32)
    sums_f = [column_sum(grad_normed * normed), column_sum(grad_normed), column_sum(grad_out)]
    grad = (grad_out + norm_back(grad_normed, normed, scale, vec_ref[1:2])).astype(BF)

    grad_out = grad.astype(F32)
    for s in range(SEC):
        gw_ref[s, :, 384:512] = dot_tn(mixed, grad[:, 128 * s : 128 * s + 128]).astype(BF)
    grad_mixed = dot_nt(grad, w_out).astype(BF)
    grad_packed = attention_bwd(packed, grad_mixed, 512, 32, 196, p_ref)
    grad_normed = jnp.zeros((DEC_ROWS, 512), F32)
    for s in range(SEC):
        part = grad_packed[:, 384 * s : 384 * s + 384]
        gw_ref[s, :, 0:384] = dot_tn(low_a, part).astype(BF)
        grad_normed = grad_normed + dot_nt(part, w_ref[s, :, 0:384])
    give((1024, 512), rows_place(gw_ref, 64))
    grad_placed = grad_out + norm_back(grad_normed, normed_a, scale_a, vec_ref[0:1])
    grad_token = column_sum(uncovered * grad_placed)
    grad_embedded = lax.dot_general(
        onehot, grad_placed, (((0,), (0,)), ((), ())), precision=lax.Precision.HIGHEST, preferred_element_type=F32
    ).astype(BF)
    for s in range(SEC):
        ge_ref[s] = dot_tn(before, grad_embedded[:, 128 * s : 128 * s + 128]).astype(BF)
    give((1536, 128), part_place(ge_ref, 0, 64))
    give((1664, 128), part_place(ge_ref, 64, 32), 32)
    dx_ref[...] = dot_nt(grad_embedded, jnp.concatenate([e_ref[s] for s in range(SEC)], axis=1)).astype(BF)
    totals = column_sum(grad_packed.astype(F32))
    gvec_ref[...] = jnp.concatenate(
        [
            column_sum(grad_normed * normed_a),
            sums_f[0],
            column_sum(grad_embedded.astype(F32)),
            grad_token,
            column_sum(grad_normed),
            totals[:, :512],
            totals[:, 1024:],
            column_sum(grad_out),
            *sums_f[1:],
        ],
        axis=0,
    )
    wait_all(copies)


def enc_ffn_bwd(inn, table, dh_ref, h_ref, a_ref, r_ref, vec_ref, *refs):
    (ups, downs), rest = take(refs, inn)
    dx_ref, gvec_ref, gupb_ref, *rest = rest
    (sends,), (u_ref, v_ref, dr_ref, df_ref, sem_u, sem_v) = take(rest, ((SEC, 0),))
    copies_v = []
    for half in range(2):
        copies_v += block_copies(
            downs, table, inn[1][1], (0, 96), (384 * half, 384), turned_place(v_ref, 192, 384, 96 * half, 96), sem_v
        )
    copies_u = block_copies(ups, table, inn[0][1], (0, 96), (0, 768), rows_place(u_ref, 96), sem_u)
    grad = dh_ref[...]
    grad_out = grad.astype(F32)
    low = a_ref[...]
    for s in range(SEC):
        df_ref[s] = grad[:, 192 * s : 192 * s + 192]
        sends[s][:, 0:768] = low
    wait_all(copies_v)
    wait_all(copies_u)
    grad_normed = jnp.zeros((ENC_ROWS, 768), F32)
    for s in range(SEC):
        lanes = slice(768 * s, 768 * s + 768)
        hidden = r_ref[:, lanes]
        active, share = gelu_parts(hidden)
        active = active.astype(BF)
        for r in range(SEC):
            sends[r][:, 768 + 768 * s : 1536 + 768 * s] = active
        grad_hidden = (dot(grad, v_ref[:, lanes]) * gelu_slope(hidden, share)).astype(BF)
        gupb_ref[:, lanes] = column_sum(grad_hidden.astype(F32))
        dr_ref[s] = grad_hidden
        grad_normed = grad_normed + dot_nt(grad_hidden, u_ref[s])
    here = table[SECTION]
    for r in range(SEC):
        sends[r][:, 3840:4608] = dr_ref[here ^ r]
        sends[r][:, 4608:4800] = df_ref[here ^ r]
    normed, scale = norm_stats(h_ref[...].astype(F32))
    gvec_ref[...] = jnp.concatenate(
        [column_sum(grad_normed * normed), column_sum(grad_normed), column_sum(grad_out)], axis=0
    )
    dx_ref[...] = (grad_out + norm_back(grad_normed, normed, scale, vec_ref[1:2])).astype(BF)


def enc_att_bwd(inn, table, dh_ref, x_ref, a_ref, k_ref, z_ref, vec_ref, ge_ref, gue_ref, gd_ref, gud_ref, *refs):
    (pieces,), (dx_ref, *rest) = take(refs, inn)
    (sends,), (w_ref, d_ref, v_ref, sem_w) = take(rest, ((SEC, 0),))
    copies_w = block_copies(pieces, table, inn[0][1], (0, 96), (0, 768), rows_place(w_ref, 96), sem_w)
    grad = dh_ref[...]
    grad_out = grad.astype(F32)
    low, packed, mixed = a_ref[...], k_ref[...], z_ref[...]
    gap = jnp.zeros((ENC_ROWS, 64), BF)
    parts = [grad[:, 192 * s : 192 * s + 192] for s in range(SEC)]
    wait_all(copies_w)
    grad_mixed = jnp.zeros((ENC_ROWS, 768), F32)
    for s in range(SEC):
        grad_mixed = grad_mixed + dot_nt(jnp.concatenate([gap, parts[s]], axis=1), w_ref[s, :, 512:768])
    grad_packed = attention_bwd(packed, grad_mixed.astype(BF), 768, 64, 49, None)
    grad_normed = jnp.zeros((ENC_ROWS, 768), F32)
    for s in range(SEC):
        part = grad_packed[:, 576 * s : 576 * s + 576]
        d_ref[s] = jnp.concatenate([part, parts[s]], axis=1)
        grad_normed = grad_normed + dot_nt(jnp.concatenate([part, gap], axis=1), w_ref[s, :, 0:640])
    normed, scale = norm_stats(padded(x_ref[0].astype(F32), ENC_ROWS))
    grad_in = grad_out + norm_back(grad_normed, normed, scale, vec_ref[0:1])
    dx_ref[0] = grad_in[:49]
    totals = column_sum(grad_packed.astype(F32))
    others, dec = ge_ref[...], gd_ref[...]
    enc = jnp.concatenate(
        [
            column_sum(grad_normed * normed), others[:1], column_sum(grad_normed), totals[:, :768],
            totals[:, 1536:], column_sum(grad_out), others[1:],
        ],
        axis=0,
    )
    tail = jnp.concatenate([dec[8:], jnp.zeros((6, 512), F32)], axis=0)
    dec = dec[:8]
    up_e = jnp.concatenate([gue_ref[...], jnp.zeros((7, 3072), F32)], axis=0)
    up_d = jnp.concatenate([gud_ref[...], jnp.zeros((7, 2048), F32)], axis=0)
    v_ref[...] = jnp.zeros_like(v_ref)
    for s in range(SEC):
        v_ref[s, :, 0:192] = enc[:, 192 * s : 192 * s + 192]
        v_ref[s, :, 256:384] = dec[:, 128 * s : 128 * s + 128]
        v_ref[s, :, 384:512] = tail[:, 128 * s : 128 * s + 128]
        v_ref[s, :, 512:1280] = up_e[:, 768 * s : 768 * s + 768]
        v_ref[s, :, 1280:1792] = up_d[:, 512 * s : 512 * s + 512]
    here = table[SECTION]
    for r in range(SEC):
        sends[r][:48, 0:768] = low[:48]
        sends[r][:48, 768:1536] = mixed[:48]
        sends[r][:48, 1536:2304] = d_ref[here ^ r, :48]
        last = jnp.concatenate([low[48:56], mixed[48:56], d_ref[here ^ r, 48:56]], axis=1).astype(F32)
        sends[r][48:, :] = jnp.concatenate([last, v_ref[here ^ r]], axis=0).astype(BF)


def enc_ffn_weights(outs, table, own_ref, *refs):
    (others, grads), (gu_ref, gv_ref, sem) = take(refs, ((SEC - 1, 0), outs))

    def gathered(first, count):
        return jnp.concatenate([own_ref[:, first : first + count]] + [o[:, first : first + count] for o in others], axis=0)

    turned = gathered(4608, 192)
    whole = dot_tn(gathered(0, 768), gathered(3840, 768)).astype(BF)
    for d in range(ROWB):
        gu_ref[d] = whole[96 * d : 96 * d + 96]
    copies = block_copies(grads, table, outs[1], (0, 96), (0, 768), lambda block: gu_ref.at[block], sem, True)
    for d in range(ROWB):
        gv_ref[d] = dot_tn(turned, gathered(768 + 384 * d, 384)).astype(BF)
    for half in range(2):
        copies += block_copies(
            grads, table, outs[1], (0, 96), (768 + 384 * half, 384),
            lambda block: gv_ref.at[block, pl.ds(96 * half, 96), :], sem, True,
        )
    wait_all(copies)


def enc_att_weights(outs, table, own_ref, *refs):
    (others, grads), (g_ref, v_ref, sem) = take(refs, ((SEC - 1, 0), outs))

    valid = row_mask(ENC_ROWS, 49)

    def gathered(first, count):
        return jnp.concatenate([o[:, first : first + count] for o in (own_ref, *others)], axis=0)

    def left(first):
        parts = [o[:, first : first + 768].astype(F32) for o in (own_ref, *others)]
        return jnp.concatenate([jnp.where(valid, part, 0.0).astype(BF) for part in parts], axis=0)

    right = gathered(1536, 768)
    lane = lax.broadcasted_iota(jnp.int32, (1, 768), 1)
    whole = jnp.where(lane < 576, dot_tn(left(0), right), dot_tn(left(768), right)).astype(BF)
    vectors = own_ref[48:, :1792].astype(F32)
    for other in others:
        vectors = vectors + other[48:, :1792].astype(F32)
    vectors = jnp.concatenate([vectors[8:], jnp.zeros((8, 1792), F32)], axis=0)
    below = jnp.zeros((16, 768), F32)
    for d in range(ROWB):
        g_ref[d, :96] = whole[96 * d : 96 * d + 96]
        v_ref[...] = below
        v_ref[:, 0:24] = vectors[:, 24 * d : 24 * d + 24]
        v_ref[:, 128:144] = vectors[:, 256 + 16 * d : 272 + 16 * d]
        v_ref[:, 256:272] = vectors[:, 384 + 16 * d : 400 + 16 * d]
        v_ref[:, 384:480] = vectors[:, 512 + 96 * d : 608 + 96 * d]
        v_ref[:, 512:576] = vectors[:, 1280 + 64 * d : 1344 + 64 * d]
        g_ref[d, 96:112] = v_ref[...].astype(BF)
    wait_all(block_copies(grads, table, outs[1], (0, 112), (0, 768), lambda block: g_ref.at[block], sem, True))


def pack_first(qkv_ref, out_ref, eg_ref, eb_ref, eu_ref, dg_ref, db_ref, du_ref, o_ref):
    o_ref[:96] = jnp.concatenate([qkv_ref[...], out_ref[...]], axis=1).astype(BF)
    def wide(values):
        return jnp.concatenate([values, jnp.zeros((values.shape[0], 128 - values.shape[1]), F32)], axis=1)

    def tall(values):
        return jnp.concatenate([values, jnp.zeros((8 - values.shape[0], 128), F32)], axis=0)

    db = db_ref[...]
    parts = [
        jnp.concatenate([wide(eg_ref[...]), wide(eb_ref[...])], axis=0),
        tall(jnp.concatenate([wide(eu_ref[...]), wide(du_ref[...])], axis=0)),
        jnp.concatenate([wide(dg_ref[...]), wide(db[:6])], axis=0),
        tall(wide(db[6:])),
    ]
    below = jnp.concatenate(parts + [jnp.zeros((8, 256), F32)], axis=1)
    o_ref[96:112] = jnp.concatenate([below, jnp.zeros((8, 768), F32)], axis=0).astype(BF)


def pack_rest(up_ref, down_ref, embed_ref, qkv_ref, out_ref, upd_ref, downd_ref, up_o, down_o, dec_o):
    up_o[...] = up_ref[...].astype(BF)
    turned = jnp.transpose(down_ref[...])
    down_o[...] = jnp.concatenate([turned[:96], turned[96:]], axis=1).astype(BF)
    turned = jnp.transpose(downd_ref[...])
    dec_o[...] = jnp.concatenate(
        [qkv_ref[...], out_ref[...], upd_ref[...], turned[:64], turned[64:], embed_ref[:64], padded(embed_ref[64:], 64)],
        axis=1,
    ).astype(BF)


def call(body, outs, scratch, *operands, memory, micros=8):
    spaces = {"v": pltpu.VMEM, "s": pltpu.SMEM, "h": pl.ANY}
    return pl.pallas_call(
        body,
        out_shape=[jax.ShapeDtypeStruct(shape, dtype) for shape, dtype, _ in outs],
        in_specs=[pl.BlockSpec(memory_space=spaces[m]) for m in memory],
        out_specs=[pl.BlockSpec(memory_space=spaces[m]) for _, _, m in outs],
        scratch_shapes=scratch,
        compiler_params=pltpu.CompilerParams(vmem_limit_bytes=VMEM_BYTES),
        cost_estimate=pl.CostEstimate(flops=micros * 10**9, bytes_accessed=micros * 10**6, transcendentals=0),
    )(*operands)


def fold_rows(matrix):
    half = matrix.shape[-2] // 2
    return jnp.concatenate([matrix[..., :half, :], matrix[..., half:, :]], axis=-1)


def unfold_rows(matrix):
    half = matrix.shape[-1] // 2
    return jnp.concatenate([matrix[..., :half], matrix[..., half:]], axis=-2)


def turn(matrix):
    return jnp.swapaxes(matrix, -1, -2)


def pack_weights(qkv_e, out_e, up_e, down_e, embed, qkv_d, out_d, up_d, down_d):
    return (
        jnp.concatenate([qkv_e, out_e], axis=-1),
        up_e,
        fold_rows(turn(down_e)),
        jnp.concatenate(
            [
                *(member[..., :64, :] for member in (qkv_d, out_d, up_d, fold_rows(turn(down_d)), embed)),
                jnp.pad(embed[..., 64:, :], ((0, 0), (0, 32), (0, 0))),
            ],
            axis=-1,
        ),
    )


def unpack_grads(dec, ffn_e, att_e):
    embed = jnp.concatenate([dec[..., 1536:1664], dec[..., :32, 1664:]], axis=-2)
    return (
        att_e[..., :96, :576],
        att_e[..., :96, 576:],
        ffn_e[..., :768],
        turn(unfold_rows(ffn_e[..., 768:])),
        embed,
        dec[..., 1024:1408],
        dec[..., 1408:1536],
        dec[..., :512],
        turn(unfold_rows(dec[..., 512:1024])),
    )


def spread(rows):
    return rows.transpose(1, 0, 2).reshape(rows.shape[1], -1)


def exchange(value, flip):
    flips = flip if isinstance(flip, tuple) else (flip, flip)
    pairs = [(device, device ^ flips[device & 1]) for device in range(BLOCKS)]
    return lax.ppermute(value, ("section", "dp"), pairs)


CORE, NEAR, FAR, FIRST, SECOND = 1, 2, 4, (8, 16), (16, 8)


def block_at(device, core, relative):
    first = jnp.where(core == 1, FIRST[1], FIRST[0])
    flips = NEAR * (relative & 3) + first * ((relative >> 2) & 1) + (24 - first) * ((relative >> 3) & 1)
    return ((device & 30) | core) ^ flips


EVENTS = """
aZ1 aZ2 aZ3 aC aP aQ bZ1 bZ2 bZ3 bC a1 aR bP bQ cZ1 cZ2 cZ3 a2 a3 cC b1 bR cP cQ a4 F1 b2 b3 cR b4 c1 c2 c3 c4
"""


class Order:
    def __init__(self):
        self.token = None

    def after(self, value):
        if self.token is None:
            return value
        return lax.optimization_barrier((value, self.token))[0]

    def came(self, value):
        value = self.after(value)
        self.token = value
        return value


def add(*members):
    total = members[0].astype(F32)
    for member in members[1:]:
        total = total + member.astype(F32)
    return total


def line_add(*members):
    return add(*(member[:2] for member in members)), add(*(member[2:] for member in members)).astype(BF)


def move(value, pairs):
    return lax.ppermute(value, ("section", "dp"), pairs)


MIDDLE = [(d, d ^ 6) for d in range(BLOCKS) if (d >> 1) & 3 in (1, 2)]
INWARD = [(d, d ^ 2) for d in range(BLOCKS) if (d >> 1) & 3 in (0, 3)]


def together(*members):
    return lax.optimization_barrier(members)


def shards(visible, cotangent, keep_index, positions, *parameters):
    both = ("section", "dp")
    fast = lax.axis_size("dp") == ROWB
    section = lax.axis_index("section")
    enc_g, enc_b, enc_u, dec_g, dec_b, dec_u = parameters[9:]
    enc_u, dec_u = enc_u[None], dec_u[None]
    order = jnp.arange(BLOCKS, dtype=jnp.int32)
    dma = pltpu.SemaphoreType.DMA
    enc_shape, dec_shape = (ENC_ROWS, 768), (DEC_ROWS, 512)
    enc_sq, enc_wide, dec_sq, dec_wide = (
        pltpu.VMEM(shape, BF) for shape in ((SEC, 768, 768), (768, 3072), (SEC, 512, 512), (512, 2048))
    )
    path, plain, here = order, order, section[None]
    out_path, out_z = order, order[:ROWB]
    if fast:
        device = lax.axis_index(both)
        core = device & 1
        near = jnp.where(order < 16, core, 1 - core)
        path = block_at(device, near, order & 15)
        z = (device >> 1) & 3
        line = order & 3
        line = z ^ jnp.where(line < 2, line, jnp.where((z == 0) | (z == 3), line, 5 - line))
        out_path = (block_at(device, 1 - near, 12 - (order & 12)) & 25) | (2 * line)
        out_z = (2 * line | jnp.where(order < 4, 1 - core, core))[:ROWB]
    table = jnp.concatenate([path, plain, out_path, out_z, here])
    step = Order()

    def start(member, flip):
        return exchange(step.after(member), flip)

    def spaces(*sets):
        return "h" * sum(len(member) for member, _ in sets)

    def used(*sets):
        return tuple((len(member), first) for member, first in sets)

    def operands(*sets):
        return [piece for member, _ in sets for piece in member]

    def run_f1(att_e, inputs, enc_vec=None):
        outs = [(enc_shape, BF, "v"), (enc_shape, BF, "v"), ((ENC_ROWS, 2304), BF, "v"), (enc_shape, BF, "v")]
        vectors = [((r, c), F32, "v") for r, c in ((8, 768), (1, 3072), (10, 512), (1, 2048))]
        if enc_vec is None:
            return call(
                partial(enc_att_fwd, used(att_e)),
                outs + vectors,
                [enc_sq, pltpu.VMEM((BLOCKS, 16, 512), BF), dma, dma],
                table, inputs, *operands(att_e),
                memory="sv" + spaces(att_e),
            )

        def body(table, x_ref, vec_ref, *refs):
            count = len(operands(att_e))
            enc_att_fwd(used(att_e), table, x_ref, *refs[: count + 4], vec_ref, *refs[count + 4 :])

        return call(
            body, outs, [enc_sq, dma], table, inputs, enc_vec, *operands(att_e), memory="svv" + spaces(att_e)
        )

    def run_f2(h1, up_e, down_e, enc_vec, enc_upb):
        return call(
            partial(enc_ffn_fwd, used(up_e, down_e)),
            [(enc_shape, BF, "v"), (enc_shape, BF, "v"), ((ENC_ROWS, 3072), F32, "v")],
            [enc_sq, enc_wide, dma, dma],
            table, h1, enc_vec, enc_upb, *operands(up_e, down_e),
            memory="svvv" + spaces(up_e, down_e),
        )

    if fast:
        qkv_e, out_e, mat_up, mat_down, embed, qkv_d, out_d, up_d, down_d = parameters[:9]
        (first,) = call(
            pack_first, [((112, 768), BF, "v")], [],
            qkv_e, out_e, enc_g, enc_b, enc_u, dec_g, dec_b, dec_u, memory="v" * 8,
        )
        rest = call(
            pack_rest, [((96, 768), BF, "v"), ((96, 768), BF, "v"), ((64, 1792), BF, "v")], [],
            mat_up, mat_down, embed, qkv_d, out_d, up_d, down_d, memory="v" * 7,
        )
        dec = ([lax.all_gather(rest[2], both, axis=0, tiled=False)], IN_PLAIN)
        own = {"a": first[None], "b": rest[0][None], "c": rest[1][None]}
        got = {}

        def pieces(name):
            return ([got[name + part] for part in ("C", "P", "Q", "R", "1", "2", "3", "4")], IN_PATH)

        for event in EVENTS.split():
            name, part = event[0], event[1:]
            if event == "F1":
                got[event] = list(run_f1(pieces("a"), step.after(visible)))
                got[event][0] = step.came(got[event][0])
            elif part[0] == "Z":
                got[event] = start(own[name], NEAR * int(part[1]))
            elif part == "C":
                got[event] = step.came(jnp.concatenate([own[name]] + [got[name + "Z" + i] for i in "123"], axis=0))
            elif part == "P":
                got[event] = start(got[name + "C"], FIRST)
            elif part == "Q":
                got[event] = start(got[name + "C"], SECOND)
            elif part == "R":
                got[event] = exchange(step.came(got[name + "P"]), SECOND)
            elif part in "1234":
                held = name + "CPQR"[int(part) - 1]
                got[event] = exchange(step.came(got[held]), CORE)
        att_e, up_e, down_e = pieces("a"), pieces("b"), pieces("c")
        h1, a1, k1, z1, enc_vec, enc_upb, dec_vec, dec_upb = got["F1"]
    else:
        full = []
        for member in parameters[:9]:
            member = lax.all_gather(member.astype(BF), "dp", axis=0, tiled=True)
            member = lax.all_gather(member, "section", axis=0, tiled=False)
            full.append(member.reshape(BLOCKS, member.shape[1] // ROWB, member.shape[2]))
        att_e, up_e, down_e, dec = (([member], IN_PLAIN) for member in pack_weights(*full))
        enc_vec, enc_upb, dec_vec, dec_upb = (
            lax.all_gather(member.astype(BF), both, axis=1, tiled=True).astype(F32)
            for member in (jnp.concatenate([enc_g, enc_b]), enc_u, jnp.concatenate([dec_g, dec_b]), dec_u)
        )
        h1, a1, k1, z1 = run_f1(att_e, visible, enc_vec)
    h2, a2, r2 = run_f2(h1, up_e, down_e, enc_vec, enc_upb)
    many = 2 if fast else 1

    def grad_blocks(blocks, rows, columns):
        return [((blocks // many, rows, columns), BF, "h")] * many

    embed_sq, probs = pltpu.VMEM((SEC, 768, 128), BF), pltpu.VMEM((2, 8 * DEC_ROWS, DEC_ROWS), F32)
    block_out, dh2, gvec_d, gupb_d, *g_dec = call(
        partial(dec_both, used(dec), (many, OUT_PATH)),
        [((1, 196, 512), F32, "v"), (enc_shape, BF, "v"), ((10, 512), F32, "v"), ((1, 2048), F32, "v")]
        + grad_blocks(BLOCKS, 64, 1792),
        [embed_sq, dec_sq, dec_sq, dec_wide] * 2 + [probs] + [dma] * 5,
        table, h2, keep_index, positions, cotangent, dec_vec, dec_upb, *operands(dec),
        memory="svvvvvv" + spaces(dec),
    )
    if fast:
        swap_d = exchange(g_dec[0], CORE)
    dh1, gv_ffn_e, gupb_e, *sends_f = call(
        partial(enc_ffn_bwd, used(up_e, down_e)),
        [(enc_shape, BF, "v"), ((3, 768), F32, "v"), ((1, 3072), F32, "v")] + [((ENC_ROWS, 4800), BF, "v")] * SEC,
        [enc_sq, enc_wide, pltpu.VMEM((SEC, ENC_ROWS, 768), BF), pltpu.VMEM((SEC, ENC_ROWS, 192), BF), dma, dma],
        table, dh2, h1, a2, r2, enc_vec, *operands(up_e, down_e),
        memory="s" + "v" * 5 + spaces(up_e, down_e),
    )

    def to_section(members):
        return [
            lax.ppermute(members[i], "section", [(s, s ^ i) for s in range(SEC)]) for i in range(1, SEC)
        ]

    if fast:
        dh1, swap_d, *sends_f = together(dh1, swap_d, *sends_f)
        came_f = to_section(sends_f)
        pair_d = add(g_dec[1][:8], swap_d[:8]).astype(BF)
        dh1, pair_d = together(dh1, pair_d)
        second_d = exchange(pair_d, SECOND)
    else:
        came_f = to_section(sends_f)
    input_grad, *sends_a = call(
        partial(enc_att_bwd, used(att_e)),
        [((1, 49, 768), F32, "v")] + [((ENC_ROWS, 2304), BF, "v")] * SEC,
        [enc_sq, pltpu.VMEM((SEC, ENC_ROWS, 768), BF), pltpu.VMEM((SEC, 8, 2304), F32), dma],
        table, dh1, visible, a1, k1, z1, enc_vec, gv_ffn_e, gupb_e, gvec_d, gupb_d, *operands(att_e),
        memory="s" + "v" * 10 + spaces(att_e),
    )
    step = Order()
    if fast:
        step.came(input_grad)
        second_d = step.came(second_d)
        first_d = exchange(add(g_dec[1][8:12], swap_d[8:12], second_d[:4]).astype(BF), FIRST)
        came_f = [step.came(member) for member in came_f]
        sends_a = [step.after(member) for member in sends_a]
    came_a = to_section(sends_a)
    g_ffn_e = call(
        partial(enc_ffn_weights, (many, OUT_Z)),
        grad_blocks(ROWB, 96, 1536),
        [pltpu.VMEM((ROWB, 96, 768), BF), pltpu.VMEM((ROWB, 192, 384), BF), dma],
        table, sends_f[0], *came_f,
        memory="svvvv",
    )
    if fast:
        swap_f = exchange(g_ffn_e[0], CORE)
        step.came(g_ffn_e[1])
        first_d = step.came(first_d)
        pair_d, far_d = line_add(g_dec[1][12:], swap_d[12:], second_d[4:], first_d)
        in_d = move(far_d, INWARD)
        swap_f = step.came(swap_f)
        pair_f, far_f = line_add(g_ffn_e[1], swap_f)
        in_f = move(far_f, INWARD)
        far_d = add(far_d, step.came(in_d)).astype(BF)
        mid_d = move(far_d, MIDDLE)
        came_a = [step.came(member) for member in came_a]
    g_att_e = call(
        partial(enc_att_weights, (many, OUT_Z)),
        grad_blocks(ROWB, 112, 768),
        [pltpu.VMEM((ROWB, 112, 768), BF), pltpu.VMEM((16, 768), F32), dma],
        table, sends_a[0], *came_a,
        memory="svvvv",
    )
    if fast:
        swap_x = exchange(g_att_e[0], CORE)
        step.came(g_att_e[1])
        far_f = add(far_f, step.came(in_f)).astype(BF)
        mid_f = move(far_f, MIDDLE)
        pair_d = add(pair_d, step.came(mid_d))
        near_d = exchange(pair_d[1].astype(BF), NEAR)
        swap_x = step.came(swap_x)
        pair_x, far_x = line_add(g_att_e[1], swap_x)
        in_x = move(far_x, INWARD)
        pair_f = add(pair_f, step.came(mid_f))
        near_f = exchange(pair_f[1].astype(BF), NEAR)
        far_x = add(far_x, step.came(in_x)).astype(BF)
        mid_x = move(far_x, MIDDLE)
        sum_d = add(pair_d[0], step.came(near_d))
        pair_x = add(pair_x, step.came(mid_x))
        near_x = exchange(pair_x[1].astype(BF), NEAR)
        sum_f = add(pair_f[0], step.came(near_f))
        sums = [sum_d, sum_f, add(pair_x[0], near_x)]
        matrix_outs = unpack_grads(*sums)
        below = sums[2][None, 96:104]
    else:
        matrix_outs = []
        for number, member in enumerate(unpack_grads(g_dec[0], g_ffn_e[0], g_att_e[0])):
            if number >= 4:
                member = member.reshape(SEC, ROWB * member.shape[1], member.shape[2])
                member = lax.psum_scatter(member, "section", scatter_dimension=0, tiled=False)
            else:
                member = member.reshape(ROWB * member.shape[1], member.shape[2])
            matrix_outs.append(lax.psum_scatter(member, "dp", scatter_dimension=0, tiled=True).astype(F32))
        below = g_att_e[0][:, 96:104].astype(F32)
    vector_outs = [
        spread(member)
        for member in (
            below[:, :, :24], below[:, :, 128:144], below[:, :2, 256:272], below[:, :1, 384:480], below[:, :1, 512:576]
        )
    ]
    if not fast:
        vector_outs = [lax.psum_scatter(member, "dp", scatter_dimension=1, tiled=True) for member in vector_outs]
    enc, dec_first, dec_last, enc_u, dec_u = vector_outs
    dec_all = jnp.concatenate([dec_first, dec_last], axis=0)
    return (block_out, input_grad, *matrix_outs, enc[:2], enc[2:], enc_u[0], dec_all[:2], dec_all[2:], dec_u[0])


def solution(mesh):
    matrix, wide, line = P("dp", "section"), P(None, ("section", "dp")), P(("section", "dp"))
    image = P(("section", "dp"), None, None)
    vectors = (wide, wide, line, wide, wide, line)
    return jax.shard_map(
        shards,
        mesh=mesh,
        in_specs=(image, image, P(("section", "dp"), None), P()) + (matrix,) * 9 + vectors,
        out_specs=(image, image) + (matrix,) * 9 + vectors,
        check_vma=False,
    )
```

```python
from functools import partial

import jax
import jax.numpy as jnp
from jax import lax
from jax.experimental import pallas as pl
from jax.experimental.pallas import tpu as pltpu
from jax.sharding import PartitionSpec as P

HE = 12
HD = 16
EPS = 1e-06
SEC = 4
ROWB = 8
BLOCKS = SEC * ROWB
ENC_ROWS = 64
DEC_ROWS = 208
BF = jnp.bfloat16
F32 = jnp.float32
IN_PATH, IN_PLAIN, OUT_PATH, OUT_Z, SECTION = 0, BLOCKS, 2 * BLOCKS, 3 * BLOCKS, 3 * BLOCKS + ROWB
VMEM_BYTES = 60 * 1024 * 1024


def dot(left, right):
    return jnp.dot(left, right, preferred_element_type=F32)


def dot_nt(left, right):
    return lax.dot_general(left, right, (((1,), (1,)), ((), ())), preferred_element_type=F32)


def dot_tn(left, right):
    return lax.dot_general(left, right, (((0,), (0,)), ((), ())), preferred_element_type=F32)


def norm_stats(values):
    centred = values - jnp.mean(values, axis=-1, keepdims=True)
    scale = lax.rsqrt(jnp.mean(centred * centred, axis=-1, keepdims=True) + EPS)
    return centred * scale, scale


def norm_back(grad, normed, scale, gain):
    inner = grad * gain
    mean_inner = jnp.mean(inner, axis=-1, keepdims=True)
    mean_cross = jnp.mean(inner * normed, axis=-1, keepdims=True)
    return scale * (inner - mean_inner - normed * mean_cross)


def column_sum(values):
    return jnp.sum(values, axis=0, keepdims=True)


def gelu_parts(values):
    share = 0.5 * (1.0 + lax.erf(values * (0.5**0.5)))
    return values * share, share


def gelu_slope(values, share):
    return share + values * (jnp.exp(-0.5 * values * values) * 0.3989422804014327)


def head_masks(width, size, dtype):
    lane = lax.broadcasted_iota(jnp.int32, (1, width), 1)
    return [
        jnp.where((lane >= h * size) & (lane < (h + 1) * size), 1.0, 0.0).astype(dtype)
        for h in range(width // size)
    ]


def stack_heads(window, size):
    return jnp.concatenate([window * m for m in head_masks(window.shape[1], size, window.dtype)], axis=0)


def unstack_heads(stacked, size):
    masks = head_masks(stacked.shape[1], size, stacked.dtype)
    rows = stacked.shape[0] // len(masks)
    total = stacked[:rows] * masks[0]
    for h in range(1, len(masks)):
        total = total + stacked[h * rows : (h + 1) * rows] * masks[h]
    return total


def softmax_rows(queries, keys, valid, size):
    scores = dot_nt(queries, keys) * size**-0.5
    lane = lax.broadcasted_iota(jnp.int32, (1, scores.shape[1]), 1)
    scores = jnp.where(lane < valid, scores, -1e30)
    powers = jnp.exp(scores - jnp.max(scores, axis=-1, keepdims=True))
    return powers / jnp.sum(powers, axis=-1, keepdims=True)


def attention_fwd(packed, width, size, valid, keep_probs):
    parts = []
    for w in range(width // 256):
        lanes = slice(256 * w, 256 * w + 256)
        queries = stack_heads(packed[:, lanes], size)
        keys = packed[:, width + 256 * w : width + 256 * w + 256]
        values = packed[:, 2 * width + 256 * w : 2 * width + 256 * w + 256]
        probs = softmax_rows(queries, keys, valid, size)
        if keep_probs is not None:
            keep_probs[w] = probs
        parts.append(unstack_heads(dot(probs.astype(BF), values), size))
    return jnp.concatenate(parts, axis=1).astype(BF)


def attention_bwd(packed, grad_mixed, width, size, valid, kept_probs):
    grad_q, grad_k, grad_v = [], [], []
    for w in range(width // 256):
        queries = stack_heads(packed[:, 256 * w : 256 * w + 256], size)
        keys = packed[:, width + 256 * w : width + 256 * w + 256]
        values = packed[:, 2 * width + 256 * w : 2 * width + 256 * w + 256]
        grads = stack_heads(grad_mixed[:, 256 * w : 256 * w + 256], size)
        probs = softmax_rows(queries, keys, valid, size) if kept_probs is None else kept_probs[w]
        grad_probs = dot_nt(grads, values)
        centre = jnp.sum(probs * grad_probs, axis=-1, keepdims=True)
        grad_scores = (probs * (grad_probs - centre)).astype(BF)
        grad_q.append(unstack_heads(dot(grad_scores, keys), size) * size**-0.5)
        grad_k.append(dot_tn(grad_scores, queries) * size**-0.5)
        grad_v.append(dot_tn(probs.astype(BF), grads))
    return jnp.concatenate(grad_q + grad_k + grad_v, axis=1).astype(BF)


def block_copies(pieces, table, first, rows, lanes, place, sem, store=False):
    copies = []
    number = first
    for piece in pieces:
        for i in range(piece.shape[0]):
            outer = piece.at[i, pl.ds(*rows), pl.ds(*lanes)]
            inner = place(table[number])
            source, target = (inner, outer) if store else (outer, inner)
            copies.append(pltpu.make_async_copy(source, target, sem))
            number += 1
    for copy in copies:
        copy.start()
    return copies


def wait_all(copies):
    for copy in copies:
        copy.wait()


def rows_place(scratch, rows):
    def place(block):
        return scratch.at[block // ROWB, pl.ds(pl.multiple_of((block % ROWB) * rows, rows), rows), :]

    return place


def turned_place(scratch, rows, columns, first, count):
    def place(block):
        top = pl.multiple_of((block // ROWB) * rows + first, count)
        return scratch.at[pl.ds(top, count), pl.ds(pl.multiple_of((block % ROWB) * columns, columns), columns)]

    return place


def part_place(scratch, first, count):
    def place(block):
        top = pl.multiple_of((block % ROWB) * 96 + first, 32)
        return scratch.at[block // ROWB, pl.ds(top, count), :]

    return place


def take(refs, sizes):
    groups = []
    for count, _ in sizes:
        groups.append(refs[:count])
        refs = refs[count:]
    return groups, refs


def padded(values, rows):
    short = rows - values.shape[0]
    return jnp.concatenate([values, jnp.zeros((short, values.shape[1]), values.dtype)], axis=0)


def row_mask(rows, valid):
    return lax.broadcasted_iota(jnp.int32, (rows, 1), 0) < valid


def unpack_vectors(rows_ref, enc_ref, upe_ref, dec_ref, upd_ref):
    def joined(first, count, width):
        parts = [rows_ref[b, :count, first : first + width].astype(F32) for b in range(BLOCKS)]
        return jnp.concatenate(parts, axis=1)

    enc_ref[...] = joined(0, 8, 24)
    upe_ref[...] = joined(128, 1, 96)
    upd_ref[...] = joined(128, 2, 64)[1:]
    dec_ref[...] = jnp.concatenate([joined(256, 8, 16), joined(384, 2, 16)], axis=0)


def enc_att_fwd(inn, table, x_ref, *refs):
    (pieces,), (h_ref, a_ref, k_ref, z_ref, *rest) = take(refs, inn)
    if len(rest) == 3:
        vec_ref, w_ref, sem = rest
        copies = block_copies(pieces, table, inn[0][1], (0, 96), (0, 768), rows_place(w_ref, 96), sem)
    else:
        vec_ref, upe_ref, dec_ref, upd_ref, w_ref, rows_ref, sem, sem_v = rest
        first = block_copies(pieces, table, inn[0][1], (96, 16), (0, 512), lambda block: rows_ref.at[block], sem_v)
        copies = block_copies(pieces, table, inn[0][1], (0, 96), (0, 768), rows_place(w_ref, 96), sem)
        wait_all(first)
        unpack_vectors(rows_ref, vec_ref, upe_ref, dec_ref, upd_ref)
    inputs = padded(x_ref[0].astype(F32), ENC_ROWS)
    normed, _ = norm_stats(inputs)
    low = (normed * vec_ref[0:1] + vec_ref[2:3]).astype(BF)
    a_ref[...] = low
    wait_all(copies)
    packed = jnp.concatenate([dot(low, w_ref[s, :, 0:640])[:, :576] for s in range(SEC)], axis=1)
    zero = jnp.zeros((1, 768), F32)
    packed = (packed + jnp.concatenate([vec_ref[3:4], zero, vec_ref[4:5]], axis=1)).astype(BF)
    k_ref[...] = packed
    mixed = attention_fwd(packed, 768, 64, 49, None)
    z_ref[...] = mixed
    result = jnp.concatenate([dot(mixed, w_ref[s, :, 512:768])[:, 64:] for s in range(SEC)], axis=1)
    h_ref[...] = (inputs + result + vec_ref[5:6]).astype(BF)


def placing(keep_ref):
    keep = jnp.concatenate([keep_ref[...], jnp.full((1, ENC_ROWS - 49), -1, jnp.int32)], axis=1)
    place = lax.broadcasted_iota(jnp.int32, (DEC_ROWS, ENC_ROWS), 0)
    return jnp.where(place == keep, 1.0, 0.0).astype(F32)


def middle(inn, outs, table, h_ref, keep_ref, pos_ref, ct_ref, enc_ref, upe_ref, dec_ref, upd_ref, *refs):
    (ups, downs, pieces), rest = take(refs, inn)
    y_ref, dx_ref, genc_ref, gupe_ref, gdec_ref, gupd_ref, *rest = rest
    (sends, grads), rest = take(rest, ((SEC, 0), outs))
    eu_ref, ev_ref, r_ref, dr_ref, df_ref, e_ref, w_ref, u_ref, v_ref, ge_ref, gw_ref, gu_ref, gv_ref, p_ref = rest[:14]
    sem_eu, sem_ev, sem_e, sem_w, sem_u, sem_v, sem_o = rest[14:]
    copies_eu = block_copies(ups, table, inn[0][1], (0, 96), (0, 768), rows_place(eu_ref, 96), sem_eu)
    copies_ev = []
    for half in range(2):
        copies_ev += block_copies(
            downs, table, inn[1][1], (0, 96), (384 * half, 384), turned_place(ev_ref, 192, 384, 96 * half, 96), sem_ev
        )
    start = inn[2][1]
    copies_e = block_copies(pieces, table, start, (0, 64), (1536, 128), part_place(e_ref, 0, 64), sem_e)
    copies_e += block_copies(pieces, table, start, (0, 32), (1664, 128), part_place(e_ref, 64, 32), sem_e)
    copies_w = block_copies(pieces, table, start, (0, 64), (0, 512), rows_place(w_ref, 64), sem_w)
    copies_u = block_copies(pieces, table, start, (0, 64), (512, 512), rows_place(u_ref, 64), sem_u)
    copies_v = []
    for half in range(2):
        copies_v += block_copies(
            pieces, table, start, (0, 64), (1024 + 256 * half, 256), turned_place(v_ref, 128, 256, 64 * half, 64), sem_v
        )
    inputs_e = h_ref[...].astype(F32)
    normed_e, scale_e = norm_stats(inputs_e)
    low_e = (normed_e * enc_ref[1:2] + enc_ref[6:7]).astype(BF)
    wait_all(copies_eu)
    active = []
    for s in range(SEC):
        lanes = slice(768 * s, 768 * s + 768)
        hidden = dot(low_e, eu_ref[s]) + upe_ref[:, lanes]
        r_ref[:, lanes] = hidden
        active.append(gelu_parts(hidden)[0].astype(BF))
        for r in range(SEC):
            sends[r][:, 768 + 768 * s : 1536 + 768 * s] = active[s]
    for r in range(SEC):
        sends[r][:, 0:768] = low_e
    wait_all(copies_ev)
    result = dot_nt(jnp.concatenate(active, axis=1), ev_ref[...])
    after_e = (inputs_e + result + enc_ref[7:8]).astype(BF)

    copies = []

    def give(lanes, place, rows=64):
        copies.extend(block_copies(grads, table, outs[1], (0, rows), lanes, place, sem_o, True))

    before = after_e
    onehot = placing(keep_ref)
    uncovered = 1.0 - jnp.sum(onehot, axis=1, keepdims=True)
    wait_all(copies_e)
    embedded = dot(before, jnp.concatenate([e_ref[s] for s in range(SEC)], axis=1)) + dec_ref[2:3]
    placed = jnp.dot(onehot, embedded, precision=lax.Precision.HIGHEST, preferred_element_type=F32)
    placed = placed + uncovered * dec_ref[3:4] + padded(pos_ref[...], DEC_ROWS)
    normed_a, scale_a = norm_stats(placed)
    low_a = (normed_a * dec_ref[0:1] + dec_ref[4:5]).astype(BF)
    wait_all(copies_w)
    packed = jnp.concatenate([dot(low_a, w_ref[s, :, 0:384]) for s in range(SEC)], axis=1)
    zero = jnp.zeros((1, 512), F32)
    packed = (packed + jnp.concatenate([dec_ref[5:6], zero, dec_ref[6:7]], axis=1)).astype(BF)
    mixed = attention_fwd(packed, 512, 32, 196, p_ref)
    w_out = jnp.concatenate([w_ref[s, :, 384:512] for s in range(SEC)], axis=1)
    inputs = (placed + dot(mixed, w_out) + dec_ref[7:8]).astype(BF).astype(F32)

    normed, scale = norm_stats(inputs)
    low = (normed * dec_ref[1:2] + dec_ref[8:9]).astype(BF)
    wait_all(copies_u)
    hidden, active = [], []
    for s in range(SEC):
        hidden.append(dot(low, u_ref[s]) + upd_ref[:, 512 * s : 512 * s + 512])
        active.append(gelu_parts(hidden[s])[0].astype(BF))
    active = jnp.concatenate(active, axis=1)
    wait_all(copies_v)
    result = inputs + dot_nt(active, v_ref[...]) + dec_ref[9:10]
    y_ref[0] = result[:196]

    grad_low = padded(ct_ref[0].astype(F32), DEC_ROWS).astype(BF)
    gv_ref[...] = dot_tn(grad_low, active).astype(BF)
    for half in range(2):
        give((512 + 256 * half, 256), turned_place(gv_ref, 128, 256, 64 * half, 64))
    grad_normed = jnp.zeros((DEC_ROWS, 512), F32)
    for s in range(SEC):
        lanes = slice(512 * s, 512 * s + 512)
        share = gelu_parts(hidden[s])[1]
        grad_hidden = (dot(grad_low, v_ref[:, lanes]) * gelu_slope(hidden[s], share)).astype(BF)
        gupd_ref[:, lanes] = column_sum(grad_hidden.astype(F32))
        gu_ref[s] = dot_tn(low, grad_hidden).astype(BF)
        grad_normed = grad_normed + dot_nt(grad_hidden, u_ref[s])
    give((0, 512), rows_place(gu_ref, 64))
    grad_out = grad_low.astype(F32)
    sums_f = [column_sum(grad_normed * normed), column_sum(grad_normed), column_sum(grad_out)]
    grad = (grad_out + norm_back(grad_normed, normed, scale, dec_ref[1:2])).astype(BF)

    grad_out = grad.astype(F32)
    for s in range(SEC):
        gw_ref[s, :, 384:512] = dot_tn(mixed, grad[:, 128 * s : 128 * s + 128]).astype(BF)
    grad_mixed = dot_nt(grad, w_out).astype(BF)
    grad_packed = attention_bwd(packed, grad_mixed, 512, 32, 196, p_ref)
    grad_normed = jnp.zeros((DEC_ROWS, 512), F32)
    for s in range(SEC):
        part = grad_packed[:, 384 * s : 384 * s + 384]
        gw_ref[s, :, 0:384] = dot_tn(low_a, part).astype(BF)
        grad_normed = grad_normed + dot_nt(part, w_ref[s, :, 0:384])
    give((1024, 512), rows_place(gw_ref, 64))
    grad_placed = grad_out + norm_back(grad_normed, normed_a, scale_a, dec_ref[0:1])
    grad_token = column_sum(uncovered * grad_placed)
    grad_embedded = lax.dot_general(
        onehot, grad_placed, (((0,), (0,)), ((), ())), precision=lax.Precision.HIGHEST, preferred_element_type=F32
    ).astype(BF)
    for s in range(SEC):
        ge_ref[s] = dot_tn(before, grad_embedded[:, 128 * s : 128 * s + 128]).astype(BF)
    give((1536, 128), part_place(ge_ref, 0, 64))
    give((1664, 128), part_place(ge_ref, 64, 32), 32)
    grad_e = dot_nt(grad_embedded, jnp.concatenate([e_ref[s] for s in range(SEC)], axis=1)).astype(BF)
    totals = column_sum(grad_packed.astype(F32))
    gdec_ref[...] = jnp.concatenate(
        [
            column_sum(grad_normed * normed_a),
            sums_f[0],
            column_sum(grad_embedded.astype(F32)),
            grad_token,
            column_sum(grad_normed),
            totals[:, :512],
            totals[:, 1024:],
            column_sum(grad_out),
            *sums_f[1:],
        ],
        axis=0,
    )

    grad_out = grad_e.astype(F32)
    for s in range(SEC):
        df_ref[s] = grad_e[:, 192 * s : 192 * s + 192]
    grad_normed = jnp.zeros((ENC_ROWS, 768), F32)
    for s in range(SEC):
        lanes = slice(768 * s, 768 * s + 768)
        hidden = r_ref[:, lanes]
        share = gelu_parts(hidden)[1]
        grad_hidden = (dot(grad_e, ev_ref[:, lanes]) * gelu_slope(hidden, share)).astype(BF)
        gupe_ref[:, lanes] = column_sum(grad_hidden.astype(F32))
        dr_ref[s] = grad_hidden
        grad_normed = grad_normed + dot_nt(grad_hidden, eu_ref[s])
    here = table[SECTION]
    for r in range(SEC):
        sends[r][:, 3840:4608] = dr_ref[here ^ r]
        sends[r][:, 4608:4800] = df_ref[here ^ r]
    genc_ref[...] = jnp.concatenate(
        [column_sum(grad_normed * normed_e), column_sum(grad_normed), column_sum(grad_out)], axis=0
    )
    dx_ref[...] = (grad_out + norm_back(grad_normed, normed_e, scale_e, enc_ref[1:2])).astype(BF)
    wait_all(copies)


def enc_att_bwd(inn, table, dh_ref, x_ref, a_ref, k_ref, z_ref, vec_ref, ge_ref, gue_ref, gd_ref, gud_ref, *refs):
    (pieces,), (dx_ref, *rest) = take(refs, inn)
    (sends,), (w_ref, d_ref, v_ref, sem_w) = take(rest, ((SEC, 0),))
    copies_w = block_copies(pieces, table, inn[0][1], (0, 96), (0, 768), rows_place(w_ref, 96), sem_w)
    grad = dh_ref[...]
    grad_out = grad.astype(F32)
    low, packed, mixed = a_ref[...], k_ref[...], z_ref[...]
    gap = jnp.zeros((ENC_ROWS, 64), BF)
    parts = [grad[:, 192 * s : 192 * s + 192] for s in range(SEC)]
    wait_all(copies_w)
    grad_mixed = jnp.zeros((ENC_ROWS, 768), F32)
    for s in range(SEC):
        grad_mixed = grad_mixed + dot_nt(jnp.concatenate([gap, parts[s]], axis=1), w_ref[s, :, 512:768])
    grad_packed = attention_bwd(packed, grad_mixed.astype(BF), 768, 64, 49, None)
    grad_normed = jnp.zeros((ENC_ROWS, 768), F32)
    for s in range(SEC):
        part = grad_packed[:, 576 * s : 576 * s + 576]
        d_ref[s] = jnp.concatenate([part, parts[s]], axis=1)
        grad_normed = grad_normed + dot_nt(jnp.concatenate([part, gap], axis=1), w_ref[s, :, 0:640])
    normed, scale = norm_stats(padded(x_ref[0].astype(F32), ENC_ROWS))
    grad_in = grad_out + norm_back(grad_normed, normed, scale, vec_ref[0:1])
    dx_ref[0] = grad_in[:49]
    totals = column_sum(grad_packed.astype(F32))
    others, dec = ge_ref[...], gd_ref[...]
    enc = jnp.concatenate(
        [
            column_sum(grad_normed * normed), others[:1], column_sum(grad_normed), totals[:, :768],
            totals[:, 1536:], column_sum(grad_out), others[1:],
        ],
        axis=0,
    )
    tail = jnp.concatenate([dec[8:], jnp.zeros((6, 512), F32)], axis=0)
    dec = dec[:8]
    up_e = jnp.concatenate([gue_ref[...], jnp.zeros((7, 3072), F32)], axis=0)
    up_d = jnp.concatenate([gud_ref[...], jnp.zeros((7, 2048), F32)], axis=0)
    v_ref[...] = jnp.zeros_like(v_ref)
    for s in range(SEC):
        v_ref[s, :, 0:192] = enc[:, 192 * s : 192 * s + 192]
        v_ref[s, :, 256:384] = dec[:, 128 * s : 128 * s + 128]
        v_ref[s, :, 384:512] = tail[:, 128 * s : 128 * s + 128]
        v_ref[s, :, 512:1280] = up_e[:, 768 * s : 768 * s + 768]
        v_ref[s, :, 1280:1792] = up_d[:, 512 * s : 512 * s + 512]
    here = table[SECTION]
    for r in range(SEC):
        sends[r][:48, 0:768] = low[:48]
        sends[r][:48, 768:1536] = mixed[:48]
        sends[r][:48, 1536:2304] = d_ref[here ^ r, :48]
        last = jnp.concatenate([low[48:56], mixed[48:56], d_ref[here ^ r, 48:56]], axis=1).astype(F32)
        sends[r][48:, :] = jnp.concatenate([last, v_ref[here ^ r]], axis=0).astype(BF)


def enc_ffn_weights(outs, table, own_ref, *refs):
    (others, grads), (gu_ref, gv_ref, sem) = take(refs, ((SEC - 1, 0), outs))

    def gathered(first, count):
        return jnp.concatenate([own_ref[:, first : first + count]] + [o[:, first : first + count] for o in others], axis=0)

    turned = gathered(4608, 192)
    whole = dot_tn(gathered(0, 768), gathered(3840, 768)).astype(BF)
    for d in range(ROWB):
        gu_ref[d] = whole[96 * d : 96 * d + 96]
    copies = block_copies(grads, table, outs[1], (0, 96), (0, 768), lambda block: gu_ref.at[block], sem, True)
    for d in range(ROWB):
        gv_ref[d] = dot_tn(turned, gathered(768 + 384 * d, 384)).astype(BF)
    for half in range(2):
        copies += block_copies(
            grads, table, outs[1], (0, 96), (768 + 384 * half, 384),
            lambda block: gv_ref.at[block, pl.ds(96 * half, 96), :], sem, True,
        )
    wait_all(copies)


def enc_att_weights(outs, table, own_ref, *refs):
    (others, grads), (g_ref, v_ref, sem) = take(refs, ((SEC - 1, 0), outs))

    valid = row_mask(ENC_ROWS, 49)

    def gathered(first, count):
        return jnp.concatenate([o[:, first : first + count] for o in (own_ref, *others)], axis=0)

    def left(first):
        parts = [o[:, first : first + 768].astype(F32) for o in (own_ref, *others)]
        return jnp.concatenate([jnp.where(valid, part, 0.0).astype(BF) for part in parts], axis=0)

    right = gathered(1536, 768)
    lane = lax.broadcasted_iota(jnp.int32, (1, 768), 1)
    whole = jnp.where(lane < 576, dot_tn(left(0), right), dot_tn(left(768), right)).astype(BF)
    vectors = own_ref[48:, :1792].astype(F32)
    for other in others:
        vectors = vectors + other[48:, :1792].astype(F32)
    vectors = jnp.concatenate([vectors[8:], jnp.zeros((8, 1792), F32)], axis=0)
    below = jnp.zeros((16, 768), F32)
    for d in range(ROWB):
        g_ref[d, :96] = whole[96 * d : 96 * d + 96]
        v_ref[...] = below
        v_ref[:, 0:24] = vectors[:, 24 * d : 24 * d + 24]
        v_ref[:, 128:144] = vectors[:, 256 + 16 * d : 272 + 16 * d]
        v_ref[:, 256:272] = vectors[:, 384 + 16 * d : 400 + 16 * d]
        v_ref[:, 384:480] = vectors[:, 512 + 96 * d : 608 + 96 * d]
        v_ref[:, 512:576] = vectors[:, 1280 + 64 * d : 1344 + 64 * d]
        g_ref[d, 96:112] = v_ref[...].astype(BF)
    wait_all(block_copies(grads, table, outs[1], (0, 112), (0, 768), lambda block: g_ref.at[block], sem, True))


def pack_first(qkv_ref, out_ref, eg_ref, eb_ref, eu_ref, dg_ref, db_ref, du_ref, o_ref):
    o_ref[:96] = jnp.concatenate([qkv_ref[...], out_ref[...]], axis=1).astype(BF)
    def wide(values):
        return jnp.concatenate([values, jnp.zeros((values.shape[0], 128 - values.shape[1]), F32)], axis=1)

    def tall(values):
        return jnp.concatenate([values, jnp.zeros((8 - values.shape[0], 128), F32)], axis=0)

    db = db_ref[...]
    parts = [
        jnp.concatenate([wide(eg_ref[...]), wide(eb_ref[...])], axis=0),
        tall(jnp.concatenate([wide(eu_ref[...]), wide(du_ref[...])], axis=0)),
        jnp.concatenate([wide(dg_ref[...]), wide(db[:6])], axis=0),
        tall(wide(db[6:])),
    ]
    below = jnp.concatenate(parts + [jnp.zeros((8, 256), F32)], axis=1)
    o_ref[96:112] = jnp.concatenate([below, jnp.zeros((8, 768), F32)], axis=0).astype(BF)


def pack_rest(up_ref, down_ref, embed_ref, qkv_ref, out_ref, upd_ref, downd_ref, up_o, down_o, dec_o):
    up_o[...] = up_ref[...].astype(BF)
    turned = jnp.transpose(down_ref[...])
    down_o[...] = jnp.concatenate([turned[:96], turned[96:]], axis=1).astype(BF)
    turned = jnp.transpose(downd_ref[...])
    dec_o[...] = jnp.concatenate(
        [qkv_ref[...], out_ref[...], upd_ref[...], turned[:64], turned[64:], embed_ref[:64], padded(embed_ref[64:], 64)],
        axis=1,
    ).astype(BF)


def call(body, outs, scratch, *operands, memory, micros=8):
    spaces = {"v": pltpu.VMEM, "s": pltpu.SMEM, "h": pl.ANY}
    return pl.pallas_call(
        body,
        out_shape=[jax.ShapeDtypeStruct(shape, dtype) for shape, dtype, _ in outs],
        in_specs=[pl.BlockSpec(memory_space=spaces[m]) for m in memory],
        out_specs=[pl.BlockSpec(memory_space=spaces[m]) for _, _, m in outs],
        scratch_shapes=scratch,
        compiler_params=pltpu.CompilerParams(vmem_limit_bytes=VMEM_BYTES),
        cost_estimate=pl.CostEstimate(flops=micros * 10**9, bytes_accessed=micros * 10**6, transcendentals=0),
    )(*operands)


def fold_rows(matrix):
    half = matrix.shape[-2] // 2
    return jnp.concatenate([matrix[..., :half, :], matrix[..., half:, :]], axis=-1)


def unfold_rows(matrix):
    half = matrix.shape[-1] // 2
    return jnp.concatenate([matrix[..., :half], matrix[..., half:]], axis=-2)


def turn(matrix):
    return jnp.swapaxes(matrix, -1, -2)


def pack_weights(qkv_e, out_e, up_e, down_e, embed, qkv_d, out_d, up_d, down_d):
    return (
        jnp.concatenate([qkv_e, out_e], axis=-1),
        up_e,
        fold_rows(turn(down_e)),
        jnp.concatenate(
            [
                *(member[..., :64, :] for member in (qkv_d, out_d, up_d, fold_rows(turn(down_d)), embed)),
                jnp.pad(embed[..., 64:, :], ((0, 0), (0, 32), (0, 0))),
            ],
            axis=-1,
        ),
    )


def unpack_grads(dec, ffn_e, att_e):
    embed = jnp.concatenate([dec[..., 1536:1664], dec[..., :32, 1664:]], axis=-2)
    return (
        att_e[..., :96, :576],
        att_e[..., :96, 576:],
        ffn_e[..., :768],
        turn(unfold_rows(ffn_e[..., 768:])),
        embed,
        dec[..., 1024:1408],
        dec[..., 1408:1536],
        dec[..., :512],
        turn(unfold_rows(dec[..., 512:1024])),
    )


def spread(rows):
    return rows.transpose(1, 0, 2).reshape(rows.shape[1], -1)


def exchange(value, flip):
    flips = flip if isinstance(flip, tuple) else (flip, flip)
    pairs = [(device, device ^ flips[device & 1]) for device in range(BLOCKS)]
    return lax.ppermute(value, ("section", "dp"), pairs)


CORE, NEAR, FAR, FIRST, SECOND = 1, 2, 4, (8, 16), (16, 8)


def block_at(device, core, relative):
    first = jnp.where(core == 1, FIRST[1], FIRST[0])
    flips = NEAR * (relative & 3) + first * ((relative >> 2) & 1) + (24 - first) * ((relative >> 3) & 1)
    return ((device & 30) | core) ^ flips


EVENTS = (
    "aZ1 aZ2 aZ3 aC",
    "aP aQ bZ1 bZ2",
    "bZ3 bC a1 aR",
    "bP bQ cZ1 cZ2",
    "cZ3 a2 a3 cC",
    "b1 bR cP cQ",
    "a4 F1 b2 b3",
    "cR b4 c1 c2",
    "c3 c4",
)


class Order:
    def __init__(self):
        self.token = None

    def after(self, value):
        if self.token is None:
            return value
        return lax.optimization_barrier((value, self.token))[0]

    def came(self, value):
        value = self.after(value)
        self.token = value
        return value


def add(*members):
    total = members[0].astype(F32)
    for member in members[1:]:
        total = total + member.astype(F32)
    return total


def line_add(*members):
    return add(*(member[:2] for member in members)), add(*(member[2:] for member in members)).astype(BF)


def move(value, pairs):
    return lax.ppermute(value, ("section", "dp"), pairs)


MIDDLE = [(d, d ^ 6) for d in range(BLOCKS) if (d >> 1) & 3 in (1, 2)]
INWARD = [(d, d ^ 2) for d in range(BLOCKS) if (d >> 1) & 3 in (0, 3)]


def together(*members):
    return lax.optimization_barrier(members)


def shards(visible, cotangent, keep_index, positions, *parameters):
    both = ("section", "dp")
    fast = lax.axis_size("dp") == ROWB
    section = lax.axis_index("section")
    enc_g, enc_b, enc_u, dec_g, dec_b, dec_u = parameters[9:]
    enc_u, dec_u = enc_u[None], dec_u[None]
    order = jnp.arange(BLOCKS, dtype=jnp.int32)
    dma = pltpu.SemaphoreType.DMA
    enc_shape, dec_shape = (ENC_ROWS, 768), (DEC_ROWS, 512)
    enc_sq, enc_wide, dec_sq, dec_wide = (
        pltpu.VMEM(shape, BF) for shape in ((SEC, 768, 768), (768, 3072), (SEC, 512, 512), (512, 2048))
    )
    path, plain, here = order, order, section[None]
    out_path, out_z = order, order[:ROWB]
    if fast:
        device = lax.axis_index(both)
        core = device & 1
        near = jnp.where(order < 16, core, 1 - core)
        path = block_at(device, near, order & 15)
        z = (device >> 1) & 3
        line = order & 3
        line = z ^ jnp.where(line < 2, line, jnp.where((z == 0) | (z == 3), line, 5 - line))
        out_path = (block_at(device, 1 - near, 12 - (order & 12)) & 25) | (2 * line)
        out_z = (2 * line | jnp.where(order < 4, 1 - core, core))[:ROWB]
    table = jnp.concatenate([path, plain, out_path, out_z, here])
    step = Order()

    def start(member, flip):
        return exchange(step.after(member), flip)

    def spaces(*sets):
        return "h" * sum(len(member) for member, _ in sets)

    def used(*sets):
        return tuple((len(member), first) for member, first in sets)

    def operands(*sets):
        return [piece for member, _ in sets for piece in member]

    def run_f1(att_e, inputs, enc_vec=None):
        outs = [(enc_shape, BF, "v"), (enc_shape, BF, "v"), ((ENC_ROWS, 2304), BF, "v"), (enc_shape, BF, "v")]
        vectors = [((r, c), F32, "v") for r, c in ((8, 768), (1, 3072), (10, 512), (1, 2048))]
        if enc_vec is None:
            return call(
                partial(enc_att_fwd, used(att_e)),
                outs + vectors,
                [enc_sq, pltpu.VMEM((BLOCKS, 16, 512), BF), dma, dma],
                table, inputs, *operands(att_e),
                memory="sv" + spaces(att_e),
            )

        def body(table, x_ref, vec_ref, *refs):
            count = len(operands(att_e))
            enc_att_fwd(used(att_e), table, x_ref, *refs[: count + 4], vec_ref, *refs[count + 4 :])

        return call(
            body, outs, [enc_sq, dma], table, inputs, enc_vec, *operands(att_e), memory="svv" + spaces(att_e)
        )

    if fast:
        qkv_e, out_e, mat_up, mat_down, embed, qkv_d, out_d, up_d, down_d = parameters[:9]
        (first,) = call(
            pack_first, [((112, 768), BF, "v")], [],
            qkv_e, out_e, enc_g, enc_b, enc_u, dec_g, dec_b, dec_u, memory="v" * 8,
        )
        rest = call(
            pack_rest, [((96, 768), BF, "v"), ((96, 768), BF, "v"), ((64, 1792), BF, "v")], [],
            mat_up, mat_down, embed, qkv_d, out_d, up_d, down_d, memory="v" * 7,
        )
        dec = ([lax.all_gather(rest[2], both, axis=0, tiled=False)], IN_PLAIN)
        own = {"a": first[None], "b": rest[0][None], "c": rest[1][None]}
        got = {}

        def pieces(name):
            return ([got[name + part] for part in ("C", "P", "Q", "R", "1", "2", "3", "4")], IN_PATH)

        for event in " ".join(EVENTS).split():
            name, part = event[0], event[1:]
            if event == "F1":
                got[event] = list(run_f1(pieces("a"), step.after(visible)))
                got[event][0] = step.came(got[event][0])
            elif part[0] == "Z":
                got[event] = start(own[name], NEAR * int(part[1]))
            elif part == "C":
                got[event] = step.came(jnp.concatenate([own[name]] + [got[name + "Z" + i] for i in "123"], axis=0))
            elif part == "P":
                got[event] = start(got[name + "C"], FIRST)
            elif part == "Q":
                got[event] = start(got[name + "C"], SECOND)
            elif part == "R":
                got[event] = exchange(step.came(got[name + "P"]), SECOND)
            elif part in "1234":
                held = name + "CPQR"[int(part) - 1]
                got[event] = exchange(step.came(got[held]), CORE)
        att_e, up_e, down_e = pieces("a"), pieces("b"), pieces("c")
        h1, a1, k1, z1, enc_vec, enc_upb, dec_vec, dec_upb = got["F1"]
    else:
        full = []
        for member in parameters[:9]:
            member = lax.all_gather(member.astype(BF), "dp", axis=0, tiled=True)
            member = lax.all_gather(member, "section", axis=0, tiled=False)
            full.append(member.reshape(BLOCKS, member.shape[1] // ROWB, member.shape[2]))
        att_e, up_e, down_e, dec = (([member], IN_PLAIN) for member in pack_weights(*full))
        enc_vec, enc_upb, dec_vec, dec_upb = (
            lax.all_gather(member.astype(BF), both, axis=1, tiled=True).astype(F32)
            for member in (jnp.concatenate([enc_g, enc_b]), enc_u, jnp.concatenate([dec_g, dec_b]), dec_u)
        )
        h1, a1, k1, z1 = run_f1(att_e, visible, enc_vec)
    many = 2 if fast else 1

    def grad_blocks(blocks, rows, columns):
        return [((blocks // many, rows, columns), BF, "h")] * many

    embed_sq, probs = pltpu.VMEM((SEC, 768, 128), BF), pltpu.VMEM((2, 8 * DEC_ROWS, DEC_ROWS), F32)
    half_sq = pltpu.VMEM((SEC, ENC_ROWS, 768), BF)
    block_out, dh1, gv_ffn_e, gupb_e, gvec_d, gupb_d, *rest = call(
        partial(middle, used(up_e, down_e, dec), (many, OUT_PATH)),
        [((1, 196, 512), F32, "v"), (enc_shape, BF, "v"), ((3, 768), F32, "v"), ((1, 3072), F32, "v")]
        + [((10, 512), F32, "v"), ((1, 2048), F32, "v")]
        + [((ENC_ROWS, 4800), BF, "v")] * SEC
        + grad_blocks(BLOCKS, 64, 1792),
        [enc_sq, enc_wide, pltpu.VMEM((ENC_ROWS, 3072), F32), half_sq, pltpu.VMEM((SEC, ENC_ROWS, 192), BF)]
        + [embed_sq, dec_sq, dec_sq, dec_wide] * 2 + [probs] + [dma] * 7,
        table, h1, keep_index, positions, cotangent, enc_vec, enc_upb, dec_vec, dec_upb, *operands(up_e, down_e, dec),
        memory="s" + "v" * 8 + spaces(up_e, down_e, dec),
    )
    sends_f, g_dec = rest[:SEC], rest[SEC:]

    def to_section(members):
        return [
            lax.ppermute(members[i], "section", [(s, s ^ i) for s in range(SEC)]) for i in range(1, SEC)
        ]

    came_f = to_section(sends_f)
    if fast:
        swap_d = exchange(g_dec[0], CORE)
    input_grad, *sends_a = call(
        partial(enc_att_bwd, used(att_e)),
        [((1, 49, 768), F32, "v")] + [((ENC_ROWS, 2304), BF, "v")] * SEC,
        [enc_sq, pltpu.VMEM((SEC, ENC_ROWS, 768), BF), pltpu.VMEM((SEC, 8, 2304), F32), dma],
        table, dh1, visible, a1, k1, z1, enc_vec, gv_ffn_e, gupb_e, gvec_d, gupb_d, *operands(att_e),
        memory="s" + "v" * 10 + spaces(att_e),
    )
    step = Order()
    if fast:
        step.came(input_grad)
        swap_d = step.came(swap_d)
        second_d = exchange(add(g_dec[1][:8], swap_d[:8]).astype(BF), SECOND)
        came_f = [step.came(member) for member in came_f]
        sends_a = [step.after(member) for member in sends_a]
    came_a = to_section(sends_a)
    g_ffn_e = call(
        partial(enc_ffn_weights, (many, OUT_Z)),
        grad_blocks(ROWB, 96, 1536),
        [pltpu.VMEM((ROWB, 96, 768), BF), pltpu.VMEM((ROWB, 192, 384), BF), dma],
        table, sends_f[0], *came_f,
        memory="svvvv",
    )
    if fast:
        swap_f = exchange(g_ffn_e[0], CORE)
        step.came(g_ffn_e[1])
        swap_f = step.came(swap_f)
        pair_f, far_f = line_add(g_ffn_e[1], swap_f)
        in_f = move(far_f, INWARD)
        came_a = [step.came(member) for member in came_a]
    g_att_e = call(
        partial(enc_att_weights, (many, OUT_Z)),
        grad_blocks(ROWB, 112, 768),
        [pltpu.VMEM((ROWB, 112, 768), BF), pltpu.VMEM((16, 768), F32), dma],
        table, sends_a[0], *came_a,
        memory="svvvv",
    )
    if fast:
        swap_x = exchange(g_att_e[0], CORE)
        step.came(g_att_e[1])
        far_f = add(far_f, step.came(in_f)).astype(BF)
        mid_f = move(far_f, MIDDLE)
        second_d = step.came(second_d)
        first_d = exchange(add(g_dec[1][8:12], swap_d[8:12], second_d[:4]).astype(BF), FIRST)
        swap_x = step.came(swap_x)
        pair_x, far_x = line_add(g_att_e[1], swap_x)
        in_x = move(far_x, INWARD)
        pair_f = add(pair_f, step.came(mid_f))
        near_f = exchange(pair_f[1].astype(BF), NEAR)
        far_x = add(far_x, step.came(in_x)).astype(BF)
        mid_x = move(far_x, MIDDLE)
        first_d = step.came(first_d)
        pair_d, far_d = line_add(g_dec[1][12:], swap_d[12:], second_d[4:], first_d)
        in_d = move(far_d, INWARD)
        pair_x = add(pair_x, step.came(mid_x))
        near_x = exchange(pair_x[1].astype(BF), NEAR)
        sum_f = add(pair_f[0], step.came(near_f))
        far_d = add(far_d, step.came(in_d)).astype(BF)
        mid_d = move(far_d, MIDDLE)
        sum_x = add(pair_x[0], step.came(near_x))
        pair_d = add(pair_d, step.came(mid_d))
        near_d = exchange(pair_d[1].astype(BF), NEAR)
        sum_d = add(pair_d[0], near_d)
        sums = [sum_d, sum_f, sum_x]
        matrix_outs = unpack_grads(*sums)
        below = sums[2][None, 96:104]
    else:
        matrix_outs = []
        for number, member in enumerate(unpack_grads(g_dec[0], g_ffn_e[0], g_att_e[0])):
            if number >= 4:
                member = member.reshape(SEC, ROWB * member.shape[1], member.shape[2])
                member = lax.psum_scatter(member, "section", scatter_dimension=0, tiled=False)
            else:
                member = member.reshape(ROWB * member.shape[1], member.shape[2])
            matrix_outs.append(lax.psum_scatter(member, "dp", scatter_dimension=0, tiled=True).astype(F32))
        below = g_att_e[0][:, 96:104].astype(F32)
    vector_outs = [
        spread(member)
        for member in (
            below[:, :, :24], below[:, :, 128:144], below[:, :2, 256:272], below[:, :1, 384:480], below[:, :1, 512:576]
        )
    ]
    if not fast:
        vector_outs = [lax.psum_scatter(member, "dp", scatter_dimension=1, tiled=True) for member in vector_outs]
    enc, dec_first, dec_last, enc_u, dec_u = vector_outs
    dec_all = jnp.concatenate([dec_first, dec_last], axis=0)
    return (block_out, input_grad, *matrix_outs, enc[:2], enc[2:], enc_u[0], dec_all[:2], dec_all[2:], dec_u[0])


def solution(mesh):
    matrix, wide, line = P("dp", "section"), P(None, ("section", "dp")), P(("section", "dp"))
    image = P(("section", "dp"), None, None)
    vectors = (wide, wide, line, wide, wide, line)
    return jax.shard_map(
        shards,
        mesh=mesh,
        in_specs=(image, image, P(("section", "dp"), None), P()) + (matrix,) * 9 + vectors,
        out_specs=(image, image) + (matrix,) * 9 + vectors,
        check_vma=False,
    )
```

```python
from functools import partial

import jax
import jax.numpy as jnp
from jax import lax
from jax.experimental import pallas as pl
from jax.experimental.pallas import tpu as pltpu
from jax.sharding import PartitionSpec as P

HE = 12
HD = 16
EPS = 1e-06
SEC = 4
ROWB = 8
BLOCKS = SEC * ROWB
ENC_ROWS = 64
DEC_ROWS = 208
BF = jnp.bfloat16
F32 = jnp.float32
IN_PATH, IN_PLAIN, OUT_PATH, OUT_Z, SECTION = 0, BLOCKS, 2 * BLOCKS, 3 * BLOCKS, 3 * BLOCKS + ROWB
VMEM_BYTES = 60 * 1024 * 1024


def dot(left, right):
    return jnp.dot(left, right, preferred_element_type=F32)


def dot_nt(left, right):
    return lax.dot_general(left, right, (((1,), (1,)), ((), ())), preferred_element_type=F32)


def dot_tn(left, right):
    return lax.dot_general(left, right, (((0,), (0,)), ((), ())), preferred_element_type=F32)


def norm_stats(values):
    centred = values - jnp.mean(values, axis=-1, keepdims=True)
    scale = lax.rsqrt(jnp.mean(centred * centred, axis=-1, keepdims=True) + EPS)
    return centred * scale, scale


def norm_back(grad, normed, scale, gain):
    inner = grad * gain
    mean_inner = jnp.mean(inner, axis=-1, keepdims=True)
    mean_cross = jnp.mean(inner * normed, axis=-1, keepdims=True)
    return scale * (inner - mean_inner - normed * mean_cross)


def column_sum(values):
    return jnp.sum(values, axis=0, keepdims=True)


def gelu_parts(values):
    share = 0.5 * (1.0 + lax.erf(values * (0.5**0.5)))
    return values * share, share


def gelu_slope(values, share):
    return share + values * (jnp.exp(-0.5 * values * values) * 0.3989422804014327)


def head_masks(width, size, dtype):
    lane = lax.broadcasted_iota(jnp.int32, (1, width), 1)
    return [
        jnp.where((lane >= h * size) & (lane < (h + 1) * size), 1.0, 0.0).astype(dtype)
        for h in range(width // size)
    ]


def stack_heads(window, size):
    return jnp.concatenate([window * m for m in head_masks(window.shape[1], size, window.dtype)], axis=0)


def unstack_heads(stacked, size):
    masks = head_masks(stacked.shape[1], size, stacked.dtype)
    rows = stacked.shape[0] // len(masks)
    total = stacked[:rows] * masks[0]
    for h in range(1, len(masks)):
        total = total + stacked[h * rows : (h + 1) * rows] * masks[h]
    return total


def softmax_rows(queries, keys, valid, size):
    scores = dot_nt(queries, keys) * size**-0.5
    lane = lax.broadcasted_iota(jnp.int32, (1, scores.shape[1]), 1)
    scores = jnp.where(lane < valid, scores, -1e30)
    powers = jnp.exp(scores - jnp.max(scores, axis=-1, keepdims=True))
    return powers / jnp.sum(powers, axis=-1, keepdims=True)


def attention_fwd(packed, width, size, valid, keep_probs):
    parts = []
    for w in range(width // 256):
        lanes = slice(256 * w, 256 * w + 256)
        queries = stack_heads(packed[:, lanes], size)
        keys = packed[:, width + 256 * w : width + 256 * w + 256]
        values = packed[:, 2 * width + 256 * w : 2 * width + 256 * w + 256]
        probs = softmax_rows(queries, keys, valid, size)
        if keep_probs is not None:
            keep_probs[w] = probs
        parts.append(unstack_heads(dot(probs.astype(BF), values), size))
    return jnp.concatenate(parts, axis=1).astype(BF)


def attention_bwd(packed, grad_mixed, width, size, valid, kept_probs):
    grad_q, grad_k, grad_v = [], [], []
    for w in range(width // 256):
        queries = stack_heads(packed[:, 256 * w : 256 * w + 256], size)
        keys = packed[:, width + 256 * w : width + 256 * w + 256]
        values = packed[:, 2 * width + 256 * w : 2 * width + 256 * w + 256]
        grads = stack_heads(grad_mixed[:, 256 * w : 256 * w + 256], size)
        probs = softmax_rows(queries, keys, valid, size) if kept_probs is None else kept_probs[w]
        grad_probs = dot_nt(grads, values)
        centre = jnp.sum(probs * grad_probs, axis=-1, keepdims=True)
        grad_scores = (probs * (grad_probs - centre)).astype(BF)
        grad_q.append(unstack_heads(dot(grad_scores, keys), size) * size**-0.5)
        grad_k.append(dot_tn(grad_scores, queries) * size**-0.5)
        grad_v.append(dot_tn(probs.astype(BF), grads))
    return jnp.concatenate(grad_q + grad_k + grad_v, axis=1).astype(BF)


def block_copies(pieces, table, first, rows, lanes, place, sem, store=False):
    copies = []
    number = first
    for piece in pieces:
        for i in range(piece.shape[0]):
            outer = piece.at[i, pl.ds(*rows), pl.ds(*lanes)]
            inner = place(table[number])
            source, target = (inner, outer) if store else (outer, inner)
            copies.append(pltpu.make_async_copy(source, target, sem))
            number += 1
    for copy in copies:
        copy.start()
    return copies


def wait_all(copies):
    for copy in copies:
        copy.wait()


def rows_place(scratch, rows):
    def place(block):
        return scratch.at[block // ROWB, pl.ds(pl.multiple_of((block % ROWB) * rows, rows), rows), :]

    return place


def turned_place(scratch, rows, columns, first, count):
    def place(block):
        top = pl.multiple_of((block // ROWB) * rows + first, count)
        return scratch.at[pl.ds(top, count), pl.ds(pl.multiple_of((block % ROWB) * columns, columns), columns)]

    return place


def part_place(scratch, first, count):
    def place(block):
        top = pl.multiple_of((block % ROWB) * 96 + first, 32)
        return scratch.at[block // ROWB, pl.ds(top, count), :]

    return place


def take(refs, sizes):
    groups = []
    for count, _ in sizes:
        groups.append(refs[:count])
        refs = refs[count:]
    return groups, refs


def padded(values, rows):
    short = rows - values.shape[0]
    return jnp.concatenate([values, jnp.zeros((short, values.shape[1]), values.dtype)], axis=0)


def row_mask(rows, valid):
    return lax.broadcasted_iota(jnp.int32, (rows, 1), 0) < valid


def unpack_vectors(rows_ref, enc_ref, upe_ref, dec_ref, upd_ref):
    def joined(first, count, width):
        parts = [rows_ref[b, :count, first : first + width].astype(F32) for b in range(BLOCKS)]
        return jnp.concatenate(parts, axis=1)

    enc_ref[...] = joined(0, 8, 24)
    upe_ref[...] = joined(128, 1, 96)
    upd_ref[...] = joined(128, 2, 64)[1:]
    dec_ref[...] = jnp.concatenate([joined(256, 8, 16), joined(384, 2, 16)], axis=0)


def enc_att_fwd(inn, table, x_ref, *refs):
    (pieces,), (h_ref, a_ref, k_ref, z_ref, *rest) = take(refs, inn)
    if len(rest) == 3:
        vec_ref, w_ref, sem = rest
        copies = block_copies(pieces, table, inn[0][1], (0, 96), (0, 768), rows_place(w_ref, 96), sem)
    else:
        vec_ref, upe_ref, dec_ref, upd_ref, w_ref, rows_ref, sem, sem_v = rest
        first = block_copies(pieces, table, inn[0][1], (96, 16), (0, 512), lambda block: rows_ref.at[block], sem_v)
        copies = block_copies(pieces, table, inn[0][1], (0, 96), (0, 768), rows_place(w_ref, 96), sem)
        wait_all(first)
        unpack_vectors(rows_ref, vec_ref, upe_ref, dec_ref, upd_ref)
    inputs = padded(x_ref[0].astype(F32), ENC_ROWS)
    normed, _ = norm_stats(inputs)
    low = (normed * vec_ref[0:1] + vec_ref[2:3]).astype(BF)
    a_ref[...] = low
    wait_all(copies)
    packed = jnp.concatenate([dot(low, w_ref[s, :, 0:640])[:, :576] for s in range(SEC)], axis=1)
    zero = jnp.zeros((1, 768), F32)
    packed = (packed + jnp.concatenate([vec_ref[3:4], zero, vec_ref[4:5]], axis=1)).astype(BF)
    k_ref[...] = packed
    mixed = attention_fwd(packed, 768, 64, 49, None)
    z_ref[...] = mixed
    result = jnp.concatenate([dot(mixed, w_ref[s, :, 512:768])[:, 64:] for s in range(SEC)], axis=1)
    h_ref[...] = (inputs + result + vec_ref[5:6]).astype(BF)


def placing(keep_ref):
    keep = jnp.concatenate([keep_ref[...], jnp.full((1, ENC_ROWS - 49), -1, jnp.int32)], axis=1)
    place = lax.broadcasted_iota(jnp.int32, (DEC_ROWS, ENC_ROWS), 0)
    return jnp.where(place == keep, 1.0, 0.0).astype(F32)


def middle(inn, outs, table, h_ref, keep_ref, pos_ref, ct_ref, enc_ref, upe_ref, dec_ref, upd_ref, *refs):
    (ups, downs, pieces), rest = take(refs, inn)
    y_ref, dx_ref, genc_ref, gupe_ref, gdec_ref, gupd_ref, *rest = rest
    (sends, grads), rest = take(rest, ((SEC, 0), outs))
    eu_ref, ev_ref, r_ref, dr_ref, df_ref, e_ref, w_ref, u_ref, v_ref, ge_ref, gw_ref, gu_ref, gv_ref, p_ref = rest[:14]
    sem_eu, sem_ev, sem_e, sem_w, sem_u, sem_v, sem_o = rest[14:]
    copies_eu = block_copies(ups, table, inn[0][1], (0, 96), (0, 768), rows_place(eu_ref, 96), sem_eu)
    copies_ev = []
    for half in range(2):
        copies_ev += block_copies(
            downs, table, inn[1][1], (0, 96), (384 * half, 384), turned_place(ev_ref, 192, 384, 96 * half, 96), sem_ev
        )
    start = inn[2][1]
    copies_e = block_copies(pieces, table, start, (0, 64), (1536, 128), part_place(e_ref, 0, 64), sem_e)
    copies_e += block_copies(pieces, table, start, (0, 32), (1664, 128), part_place(e_ref, 64, 32), sem_e)
    copies_w = block_copies(pieces, table, start, (0, 64), (0, 512), rows_place(w_ref, 64), sem_w)
    copies_u = block_copies(pieces, table, start, (0, 64), (512, 512), rows_place(u_ref, 64), sem_u)
    copies_v = []
    for half in range(2):
        copies_v += block_copies(
            pieces, table, start, (0, 64), (1024 + 256 * half, 256), turned_place(v_ref, 128, 256, 64 * half, 64), sem_v
        )
    inputs_e = h_ref[...].astype(F32)
    normed_e, scale_e = norm_stats(inputs_e)
    low_e = (normed_e * enc_ref[1:2] + enc_ref[6:7]).astype(BF)
    wait_all(copies_eu)
    active = []
    for s in range(SEC):
        lanes = slice(768 * s, 768 * s + 768)
        hidden = dot(low_e, eu_ref[s]) + upe_ref[:, lanes]
        r_ref[:, lanes] = hidden
        active.append(gelu_parts(hidden)[0].astype(BF))
        for r in range(SEC):
            sends[r][:, 768 + 768 * s : 1536 + 768 * s] = active[s]
    for r in range(SEC):
        sends[r][:, 0:768] = low_e
    wait_all(copies_ev)
    result = dot_nt(jnp.concatenate(active, axis=1), ev_ref[...])
    after_e = (inputs_e + result + enc_ref[7:8]).astype(BF)

    copies = []

    def give(lanes, place, rows=64):
        copies.extend(block_copies(grads, table, outs[1], (0, rows), lanes, place, sem_o, True))

    before = after_e
    onehot = placing(keep_ref)
    uncovered = 1.0 - jnp.sum(onehot, axis=1, keepdims=True)
    wait_all(copies_e)
    embedded = dot(before, jnp.concatenate([e_ref[s] for s in range(SEC)], axis=1)) + dec_ref[2:3]
    placed = jnp.dot(onehot, embedded, precision=lax.Precision.HIGHEST, preferred_element_type=F32)
    placed = placed + uncovered * dec_ref[3:4] + padded(pos_ref[...], DEC_ROWS)
    normed_a, scale_a = norm_stats(placed)
    low_a = (normed_a * dec_ref[0:1] + dec_ref[4:5]).astype(BF)
    wait_all(copies_w)
    packed = jnp.concatenate([dot(low_a, w_ref[s, :, 0:384]) for s in range(SEC)], axis=1)
    zero = jnp.zeros((1, 512), F32)
    packed = (packed + jnp.concatenate([dec_ref[5:6], zero, dec_ref[6:7]], axis=1)).astype(BF)
    mixed = attention_fwd(packed, 512, 32, 196, p_ref)
    w_out = jnp.concatenate([w_ref[s, :, 384:512] for s in range(SEC)], axis=1)
    inputs = (placed + dot(mixed, w_out) + dec_ref[7:8]).astype(BF).astype(F32)

    normed, scale = norm_stats(inputs)
    low = (normed * dec_ref[1:2] + dec_ref[8:9]).astype(BF)
    wait_all(copies_u)
    hidden, active = [], []
    for s in range(SEC):
        hidden.append(dot(low, u_ref[s]) + upd_ref[:, 512 * s : 512 * s + 512])
        active.append(gelu_parts(hidden[s])[0].astype(BF))
    active = jnp.concatenate(active, axis=1)
    wait_all(copies_v)
    result = inputs + dot_nt(active, v_ref[...]) + dec_ref[9:10]
    y_ref[0] = result[:196]

    grad_low = padded(ct_ref[0].astype(F32), DEC_ROWS).astype(BF)
    gv_ref[...] = dot_tn(grad_low, active).astype(BF)
    for half in range(2):
        give((512 + 256 * half, 256), turned_place(gv_ref, 128, 256, 64 * half, 64))
    grad_normed = jnp.zeros((DEC_ROWS, 512), F32)
    for s in range(SEC):
        lanes = slice(512 * s, 512 * s + 512)
        share = gelu_parts(hidden[s])[1]
        grad_hidden = (dot(grad_low, v_ref[:, lanes]) * gelu_slope(hidden[s], share)).astype(BF)
        gupd_ref[:, lanes] = column_sum(grad_hidden.astype(F32))
        gu_ref[s] = dot_tn(low, grad_hidden).astype(BF)
        grad_normed = grad_normed + dot_nt(grad_hidden, u_ref[s])
    give((0, 512), rows_place(gu_ref, 64))
    grad_out = grad_low.astype(F32)
    sums_f = [column_sum(grad_normed * normed), column_sum(grad_normed), column_sum(grad_out)]
    grad = (grad_out + norm_back(grad_normed, normed, scale, dec_ref[1:2])).astype(BF)

    grad_out = grad.astype(F32)
    for s in range(SEC):
        gw_ref[s, :, 384:512] = dot_tn(mixed, grad[:, 128 * s : 128 * s + 128]).astype(BF)
    grad_mixed = dot_nt(grad, w_out).astype(BF)
    grad_packed = attention_bwd(packed, grad_mixed, 512, 32, 196, p_ref)
    grad_normed = jnp.zeros((DEC_ROWS, 512), F32)
    for s in range(SEC):
        part = grad_packed[:, 384 * s : 384 * s + 384]
        gw_ref[s, :, 0:384] = dot_tn(low_a, part).astype(BF)
        grad_normed = grad_normed + dot_nt(part, w_ref[s, :, 0:384])
    give((1024, 512), rows_place(gw_ref, 64))
    grad_placed = grad_out + norm_back(grad_normed, normed_a, scale_a, dec_ref[0:1])
    grad_token = column_sum(uncovered * grad_placed)
    grad_embedded = lax.dot_general(
        onehot, grad_placed, (((0,), (0,)), ((), ())), precision=lax.Precision.HIGHEST, preferred_element_type=F32
    ).astype(BF)
    for s in range(SEC):
        ge_ref[s] = dot_tn(before, grad_embedded[:, 128 * s : 128 * s + 128]).astype(BF)
    give((1536, 128), part_place(ge_ref, 0, 64))
    give((1664, 128), part_place(ge_ref, 64, 32), 32)
    grad_e = dot_nt(grad_embedded, jnp.concatenate([e_ref[s] for s in range(SEC)], axis=1)).astype(BF)
    totals = column_sum(grad_packed.astype(F32))
    gdec_ref[...] = jnp.concatenate(
        [
            column_sum(grad_normed * normed_a),
            sums_f[0],
            column_sum(grad_embedded.astype(F32)),
            grad_token,
            column_sum(grad_normed),
            totals[:, :512],
            totals[:, 1024:],
            column_sum(grad_out),
            *sums_f[1:],
        ],
        axis=0,
    )

    grad_out = grad_e.astype(F32)
    for s in range(SEC):
        df_ref[s] = grad_e[:, 192 * s : 192 * s + 192]
    grad_normed = jnp.zeros((ENC_ROWS, 768), F32)
    for s in range(SEC):
        lanes = slice(768 * s, 768 * s + 768)
        hidden = r_ref[:, lanes]
        share = gelu_parts(hidden)[1]
        grad_hidden = (dot(grad_e, ev_ref[:, lanes]) * gelu_slope(hidden, share)).astype(BF)
        gupe_ref[:, lanes] = column_sum(grad_hidden.astype(F32))
        dr_ref[s] = grad_hidden
        grad_normed = grad_normed + dot_nt(grad_hidden, eu_ref[s])
    here = table[SECTION]
    for r in range(SEC):
        sends[r][:, 3840:4608] = dr_ref[here ^ r]
        sends[r][:, 4608:4800] = df_ref[here ^ r]
    genc_ref[...] = jnp.concatenate(
        [column_sum(grad_normed * normed_e), column_sum(grad_normed), column_sum(grad_out)], axis=0
    )
    dx_ref[...] = (grad_out + norm_back(grad_normed, normed_e, scale_e, enc_ref[1:2])).astype(BF)
    wait_all(copies)


def enc_att_bwd(inn, table, dh_ref, x_ref, a_ref, k_ref, z_ref, vec_ref, ge_ref, gue_ref, gd_ref, gud_ref, *refs):
    (pieces,), (dx_ref, *rest) = take(refs, inn)
    (sends,), (w_ref, d_ref, v_ref, sem_w) = take(rest, ((SEC, 0),))
    copies_w = block_copies(pieces, table, inn[0][1], (0, 96), (0, 768), rows_place(w_ref, 96), sem_w)
    grad = dh_ref[...]
    grad_out = grad.astype(F32)
    low, packed, mixed = a_ref[...], k_ref[...], z_ref[...]
    gap = jnp.zeros((ENC_ROWS, 64), BF)
    parts = [grad[:, 192 * s : 192 * s + 192] for s in range(SEC)]
    wait_all(copies_w)
    grad_mixed = jnp.zeros((ENC_ROWS, 768), F32)
    for s in range(SEC):
        grad_mixed = grad_mixed + dot_nt(jnp.concatenate([gap, parts[s]], axis=1), w_ref[s, :, 512:768])
    grad_packed = attention_bwd(packed, grad_mixed.astype(BF), 768, 64, 49, None)
    grad_normed = jnp.zeros((ENC_ROWS, 768), F32)
    for s in range(SEC):
        part = grad_packed[:, 576 * s : 576 * s + 576]
        d_ref[s] = jnp.concatenate([part, parts[s]], axis=1)
        grad_normed = grad_normed + dot_nt(jnp.concatenate([part, gap], axis=1), w_ref[s, :, 0:640])
    normed, scale = norm_stats(padded(x_ref[0].astype(F32), ENC_ROWS))
    grad_in = grad_out + norm_back(grad_normed, normed, scale, vec_ref[0:1])
    dx_ref[0] = grad_in[:49]
    totals = column_sum(grad_packed.astype(F32))
    others, dec = ge_ref[...], gd_ref[...]
    enc = jnp.concatenate(
        [
            column_sum(grad_normed * normed), others[:1], column_sum(grad_normed), totals[:, :768],
            totals[:, 1536:], column_sum(grad_out), others[1:],
        ],
        axis=0,
    )
    tail = jnp.concatenate([dec[8:], jnp.zeros((6, 512), F32)], axis=0)
    dec = dec[:8]
    up_e = jnp.concatenate([gue_ref[...], jnp.zeros((7, 3072), F32)], axis=0)
    up_d = jnp.concatenate([gud_ref[...], jnp.zeros((7, 2048), F32)], axis=0)
    v_ref[...] = jnp.zeros_like(v_ref)
    for s in range(SEC):
        v_ref[s, :, 0:192] = enc[:, 192 * s : 192 * s + 192]
        v_ref[s, :, 256:384] = dec[:, 128 * s : 128 * s + 128]
        v_ref[s, :, 384:512] = tail[:, 128 * s : 128 * s + 128]
        v_ref[s, :, 512:1280] = up_e[:, 768 * s : 768 * s + 768]
        v_ref[s, :, 1280:1792] = up_d[:, 512 * s : 512 * s + 512]
    here = table[SECTION]
    for r in range(SEC):
        sends[r][:48, 0:768] = low[:48]
        sends[r][:48, 768:1536] = mixed[:48]
        sends[r][:48, 1536:2304] = d_ref[here ^ r, :48]
        last = jnp.concatenate([low[48:56], mixed[48:56], d_ref[here ^ r, 48:56]], axis=1).astype(F32)
        sends[r][48:, :] = jnp.concatenate([last, v_ref[here ^ r]], axis=0).astype(BF)


def enc_ffn_weights(outs, table, own_ref, *refs):
    (others, grads), (gu_ref, gv_ref, sem) = take(refs, ((SEC - 1, 0), outs))

    def gathered(first, count):
        return jnp.concatenate([own_ref[:, first : first + count]] + [o[:, first : first + count] for o in others], axis=0)

    turned = gathered(4608, 192)
    whole = dot_tn(gathered(0, 768), gathered(3840, 768)).astype(BF)
    for d in range(ROWB):
        gu_ref[d] = whole[96 * d : 96 * d + 96]
    copies = block_copies(grads, table, outs[1], (0, 96), (0, 768), lambda block: gu_ref.at[block], sem, True)
    for d in range(ROWB):
        gv_ref[d] = dot_tn(turned, gathered(768 + 384 * d, 384)).astype(BF)
    for half in range(2):
        copies += block_copies(
            grads, table, outs[1], (0, 96), (768 + 384 * half, 384),
            lambda block: gv_ref.at[block, pl.ds(96 * half, 96), :], sem, True,
        )
    wait_all(copies)


def enc_att_weights(outs, table, own_ref, *refs):
    (others, grads), (g_ref, v_ref, sem) = take(refs, ((SEC - 1, 0), outs))

    valid = row_mask(ENC_ROWS, 49)

    def gathered(first, count):
        return jnp.concatenate([o[:, first : first + count] for o in (own_ref, *others)], axis=0)

    def left(first):
        parts = [o[:, first : first + 768].astype(F32) for o in (own_ref, *others)]
        return jnp.concatenate([jnp.where(valid, part, 0.0).astype(BF) for part in parts], axis=0)

    right = gathered(1536, 768)
    lane = lax.broadcasted_iota(jnp.int32, (1, 768), 1)
    whole = jnp.where(lane < 576, dot_tn(left(0), right), dot_tn(left(768), right)).astype(BF)
    vectors = own_ref[48:, :1792].astype(F32)
    for other in others:
        vectors = vectors + other[48:, :1792].astype(F32)
    vectors = jnp.concatenate([vectors[8:], jnp.zeros((8, 1792), F32)], axis=0)
    below = jnp.zeros((16, 768), F32)
    for d in range(ROWB):
        g_ref[d, :96] = whole[96 * d : 96 * d + 96]
        v_ref[...] = below
        v_ref[:, 0:24] = vectors[:, 24 * d : 24 * d + 24]
        v_ref[:, 128:144] = vectors[:, 256 + 16 * d : 272 + 16 * d]
        v_ref[:, 256:272] = vectors[:, 384 + 16 * d : 400 + 16 * d]
        v_ref[:, 384:480] = vectors[:, 512 + 96 * d : 608 + 96 * d]
        v_ref[:, 512:576] = vectors[:, 1280 + 64 * d : 1344 + 64 * d]
        g_ref[d, 96:112] = v_ref[...].astype(BF)
    wait_all(block_copies(grads, table, outs[1], (0, 112), (0, 768), lambda block: g_ref.at[block], sem, True))


def pack_first(qkv_ref, out_ref, eg_ref, eb_ref, eu_ref, dg_ref, db_ref, du_ref, o_ref):
    o_ref[:96] = jnp.concatenate([qkv_ref[...], out_ref[...]], axis=1).astype(BF)
    def wide(values):
        return jnp.concatenate([values, jnp.zeros((values.shape[0], 128 - values.shape[1]), F32)], axis=1)

    def tall(values):
        return jnp.concatenate([values, jnp.zeros((8 - values.shape[0], 128), F32)], axis=0)

    db = db_ref[...]
    parts = [
        jnp.concatenate([wide(eg_ref[...]), wide(eb_ref[...])], axis=0),
        tall(jnp.concatenate([wide(eu_ref[...]), wide(du_ref[...])], axis=0)),
        jnp.concatenate([wide(dg_ref[...]), wide(db[:6])], axis=0),
        tall(wide(db[6:])),
    ]
    below = jnp.concatenate(parts + [jnp.zeros((8, 256), F32)], axis=1)
    o_ref[96:112] = jnp.concatenate([below, jnp.zeros((8, 768), F32)], axis=0).astype(BF)


def pack_rest(up_ref, down_ref, embed_ref, qkv_ref, out_ref, upd_ref, downd_ref, up_o, down_o, dec_o):
    up_o[...] = up_ref[...].astype(BF)
    turned = jnp.transpose(down_ref[...])
    down_o[...] = jnp.concatenate([turned[:96], turned[96:]], axis=1).astype(BF)
    turned = jnp.transpose(downd_ref[...])
    dec_o[...] = jnp.concatenate(
        [qkv_ref[...], out_ref[...], upd_ref[...], turned[:64], turned[64:], embed_ref[:64], padded(embed_ref[64:], 64)],
        axis=1,
    ).astype(BF)


def call(body, outs, scratch, *operands, memory, micros=8):
    spaces = {"v": pltpu.VMEM, "s": pltpu.SMEM, "h": pl.ANY}
    return pl.pallas_call(
        body,
        out_shape=[jax.ShapeDtypeStruct(shape, dtype) for shape, dtype, _ in outs],
        in_specs=[pl.BlockSpec(memory_space=spaces[m]) for m in memory],
        out_specs=[pl.BlockSpec(memory_space=spaces[m]) for _, _, m in outs],
        scratch_shapes=scratch,
        compiler_params=pltpu.CompilerParams(vmem_limit_bytes=VMEM_BYTES),
        cost_estimate=pl.CostEstimate(flops=micros * 10**9 + 1, bytes_accessed=micros * 10**6 + 1, transcendentals=0),
    )(*operands)


def fold_rows(matrix):
    half = matrix.shape[-2] // 2
    return jnp.concatenate([matrix[..., :half, :], matrix[..., half:, :]], axis=-1)


def unfold_rows(matrix):
    half = matrix.shape[-1] // 2
    return jnp.concatenate([matrix[..., :half], matrix[..., half:]], axis=-2)


def turn(matrix):
    return jnp.swapaxes(matrix, -1, -2)


def pack_weights(qkv_e, out_e, up_e, down_e, embed, qkv_d, out_d, up_d, down_d):
    return (
        jnp.concatenate([qkv_e, out_e], axis=-1),
        up_e,
        fold_rows(turn(down_e)),
        jnp.concatenate(
            [
                *(member[..., :64, :] for member in (qkv_d, out_d, up_d, fold_rows(turn(down_d)), embed)),
                jnp.pad(embed[..., 64:, :], ((0, 0), (0, 32), (0, 0))),
            ],
            axis=-1,
        ),
    )


def unpack_grads(dec, ffn_e, att_e):
    embed = jnp.concatenate([dec[..., 1536:1664], dec[..., :32, 1664:]], axis=-2)
    return (
        att_e[..., :96, :576],
        att_e[..., :96, 576:],
        ffn_e[..., :768],
        turn(unfold_rows(ffn_e[..., 768:])),
        embed,
        dec[..., 1024:1408],
        dec[..., 1408:1536],
        dec[..., :512],
        turn(unfold_rows(dec[..., 512:1024])),
    )


def spread(rows):
    return rows.transpose(1, 0, 2).reshape(rows.shape[1], -1)


def exchange(value, flip):
    flips = flip if isinstance(flip, tuple) else (flip, flip)
    pairs = [(device, device ^ flips[device & 1]) for device in range(BLOCKS)]
    return lax.ppermute(value, ("section", "dp"), pairs)


CORE, NEAR, FAR, FIRST, SECOND = 1, 2, 4, (8, 16), (16, 8)


def block_at(device, core, relative):
    first = jnp.where(core == 1, FIRST[1], FIRST[0])
    flips = NEAR * (relative & 3) + first * ((relative >> 2) & 1) + (24 - first) * ((relative >> 3) & 1)
    return ((device & 30) | core) ^ flips


EVENTS = (
    "aZ1 aZ2 aZ3 aC",
    "aP aQ bZ1 bZ2",
    "bZ3 bC a1 aR",
    "bP bQ cZ1 cZ2",
    "cZ3 a2 a3 cC",
    "b1 bR cP cQ",
    "a4 F1 b2 b3",
    "cR b4 c1 c2",
    "c3 c4",
)


class Order:
    def __init__(self):
        self.token = None

    def after(self, value):
        if self.token is None:
            return value
        return lax.optimization_barrier((value, self.token))[0]

    def came(self, value):
        value = self.after(value)
        self.token = value
        return value


def add(*members):
    total = members[0].astype(F32)
    for member in members[1:]:
        total = total + member.astype(F32)
    return total


def line_add(*members):
    return add(*(member[:2] for member in members)), add(*(member[2:] for member in members)).astype(BF)


def move(value, pairs):
    return lax.ppermute(value, ("section", "dp"), pairs)


MIDDLE = [(d, d ^ 6) for d in range(BLOCKS) if (d >> 1) & 3 in (1, 2)]
INWARD = [(d, d ^ 2) for d in range(BLOCKS) if (d >> 1) & 3 in (0, 3)]


def together(*members):
    return lax.optimization_barrier(members)


def shards(visible, cotangent, keep_index, positions, *parameters):
    both = ("section", "dp")
    fast = lax.axis_size("dp") == ROWB
    section = lax.axis_index("section")
    enc_g, enc_b, enc_u, dec_g, dec_b, dec_u = parameters[9:]
    enc_u, dec_u = enc_u[None], dec_u[None]
    order = jnp.arange(BLOCKS, dtype=jnp.int32)
    dma = pltpu.SemaphoreType.DMA
    enc_shape, dec_shape = (ENC_ROWS, 768), (DEC_ROWS, 512)
    enc_sq, enc_wide, dec_sq, dec_wide = (
        pltpu.VMEM(shape, BF) for shape in ((SEC, 768, 768), (768, 3072), (SEC, 512, 512), (512, 2048))
    )
    path, plain, here = order, order, section[None]
    out_path, out_z = order, order[:ROWB]
    if fast:
        device = lax.axis_index(both)
        core = device & 1
        near = jnp.where(order < 16, core, 1 - core)
        path = block_at(device, near, order & 15)
        z = (device >> 1) & 3
        line = order & 3
        line = z ^ jnp.where(line < 2, line, jnp.where((z == 0) | (z == 3), line, 5 - line))
        out_path = (block_at(device, 1 - near, 12 - (order & 12)) & 25) | (2 * line)
        out_z = (2 * line | jnp.where(order < 4, 1 - core, core))[:ROWB]
    table = jnp.concatenate([path, plain, out_path, out_z, here])
    step = Order()

    def start(member, flip):
        return exchange(step.after(member), flip)

    def spaces(*sets):
        return "h" * sum(len(member) for member, _ in sets)

    def used(*sets):
        return tuple((len(member), first) for member, first in sets)

    def operands(*sets):
        return [piece for member, _ in sets for piece in member]

    def run_f1(att_e, inputs, enc_vec=None):
        outs = [(enc_shape, BF, "v"), (enc_shape, BF, "v"), ((ENC_ROWS, 2304), BF, "v"), (enc_shape, BF, "v")]
        vectors = [((r, c), F32, "v") for r, c in ((8, 768), (1, 3072), (10, 512), (1, 2048))]
        if enc_vec is None:
            return call(
                partial(enc_att_fwd, used(att_e)),
                outs + vectors,
                [enc_sq, pltpu.VMEM((BLOCKS, 16, 512), BF), dma, dma],
                table, inputs, *operands(att_e),
                memory="sv" + spaces(att_e),
            )

        def body(table, x_ref, vec_ref, *refs):
            count = len(operands(att_e))
            enc_att_fwd(used(att_e), table, x_ref, *refs[: count + 4], vec_ref, *refs[count + 4 :])

        return call(
            body, outs, [enc_sq, dma], table, inputs, enc_vec, *operands(att_e), memory="svv" + spaces(att_e)
        )

    if fast:
        qkv_e, out_e, mat_up, mat_down, embed, qkv_d, out_d, up_d, down_d = parameters[:9]
        (first,) = call(
            pack_first, [((112, 768), BF, "v")], [],
            qkv_e, out_e, enc_g, enc_b, enc_u, dec_g, dec_b, dec_u, memory="v" * 8,
        )
        rest = call(
            pack_rest, [((96, 768), BF, "v"), ((96, 768), BF, "v"), ((64, 1792), BF, "v")], [],
            mat_up, mat_down, embed, qkv_d, out_d, up_d, down_d, memory="v" * 7,
        )
        dec = ([lax.all_gather(rest[2], both, axis=0, tiled=False)], IN_PLAIN)
        own = {"a": first[None], "b": rest[0][None], "c": rest[1][None]}
        got = {}

        def pieces(name):
            return ([got[name + part] for part in ("C", "P", "Q", "R", "1", "2", "3", "4")], IN_PATH)

        for event in " ".join(EVENTS).split():
            name, part = event[0], event[1:]
            if event == "F1":
                got[event] = list(run_f1(pieces("a"), step.after(visible)))
                got[event][0] = step.came(got[event][0])
            elif part[0] == "Z":
                got[event] = start(own[name], NEAR * int(part[1]))
            elif part == "C":
                got[event] = step.came(jnp.concatenate([own[name]] + [got[name + "Z" + i] for i in "123"], axis=0))
            elif part == "P":
                got[event] = start(got[name + "C"], FIRST)
            elif part == "Q":
                got[event] = start(got[name + "C"], SECOND)
            elif part == "R":
                got[event] = exchange(step.came(got[name + "P"]), SECOND)
            elif part in "1234":
                held = name + "CPQR"[int(part) - 1]
                got[event] = exchange(step.came(got[held]), CORE)
        att_e, up_e, down_e = pieces("a"), pieces("b"), pieces("c")
        h1, a1, k1, z1, enc_vec, enc_upb, dec_vec, dec_upb = got["F1"]
    else:
        full = []
        for member in parameters[:9]:
            member = lax.all_gather(member.astype(BF), "dp", axis=0, tiled=True)
            member = lax.all_gather(member, "section", axis=0, tiled=False)
            full.append(member.reshape(BLOCKS, member.shape[1] // ROWB, member.shape[2]))
        att_e, up_e, down_e, dec = (([member], IN_PLAIN) for member in pack_weights(*full))
        enc_vec, enc_upb, dec_vec, dec_upb = (
            lax.all_gather(member.astype(BF), both, axis=1, tiled=True).astype(F32)
            for member in (jnp.concatenate([enc_g, enc_b]), enc_u, jnp.concatenate([dec_g, dec_b]), dec_u)
        )
        h1, a1, k1, z1 = run_f1(att_e, visible, enc_vec)
    many = 2 if fast else 1

    def grad_blocks(blocks, rows, columns):
        return [((blocks // many, rows, columns), BF, "h")] * many

    embed_sq, probs = pltpu.VMEM((SEC, 768, 128), BF), pltpu.VMEM((2, 8 * DEC_ROWS, DEC_ROWS), F32)
    half_sq = pltpu.VMEM((SEC, ENC_ROWS, 768), BF)
    block_out, dh1, gv_ffn_e, gupb_e, gvec_d, gupb_d, *rest = call(
        partial(middle, used(up_e, down_e, dec), (many, OUT_PATH)),
        [((1, 196, 512), F32, "v"), (enc_shape, BF, "v"), ((3, 768), F32, "v"), ((1, 3072), F32, "v")]
        + [((10, 512), F32, "v"), ((1, 2048), F32, "v")]
        + [((ENC_ROWS, 4800), BF, "v")] * SEC
        + grad_blocks(BLOCKS, 64, 1792),
        [enc_sq, enc_wide, pltpu.VMEM((ENC_ROWS, 3072), F32), half_sq, pltpu.VMEM((SEC, ENC_ROWS, 192), BF)]
        + [embed_sq, dec_sq, dec_sq, dec_wide] * 2 + [probs] + [dma] * 7,
        table, h1, keep_index, positions, cotangent, enc_vec, enc_upb, dec_vec, dec_upb, *operands(up_e, down_e, dec),
        memory="s" + "v" * 8 + spaces(up_e, down_e, dec),
    )
    sends_f, g_dec = rest[:SEC], rest[SEC:]

    def to_section(members):
        return [
            lax.ppermute(members[i], "section", [(s, s ^ i) for s in range(SEC)]) for i in range(1, SEC)
        ]

    came_f = to_section(sends_f)
    if fast:
        swap_d = exchange(g_dec[0], CORE)
    input_grad, *sends_a = call(
        partial(enc_att_bwd, used(att_e)),
        [((1, 49, 768), F32, "v")] + [((ENC_ROWS, 2304), BF, "v")] * SEC,
        [enc_sq, pltpu.VMEM((SEC, ENC_ROWS, 768), BF), pltpu.VMEM((SEC, 8, 2304), F32), dma],
        table, dh1, visible, a1, k1, z1, enc_vec, gv_ffn_e, gupb_e, gvec_d, gupb_d, *operands(att_e),
        memory="s" + "v" * 10 + spaces(att_e), micros=0,
    )
    step = Order()
    if fast:
        step.came(input_grad)
        swap_d = step.came(swap_d)
        second_d = exchange(add(g_dec[1][:8], swap_d[:8]).astype(BF), SECOND)
        came_f = [step.came(member) for member in came_f]
        sends_a = [step.after(member) for member in sends_a]
    came_a = to_section(sends_a)
    g_ffn_e = call(
        partial(enc_ffn_weights, (many, OUT_Z)),
        grad_blocks(ROWB, 96, 1536),
        [pltpu.VMEM((ROWB, 96, 768), BF), pltpu.VMEM((ROWB, 192, 384), BF), dma],
        table, sends_f[0], *came_f,
        memory="svvvv", micros=0,
    )
    if fast:
        swap_f = exchange(g_ffn_e[0], CORE)
        step.came(g_ffn_e[1])
        swap_f = step.came(swap_f)
        pair_f, far_f = line_add(g_ffn_e[1], swap_f)
        in_f = move(far_f, INWARD)
        came_a = [step.came(member) for member in came_a]
    g_att_e = call(
        partial(enc_att_weights, (many, OUT_Z)),
        grad_blocks(ROWB, 112, 768),
        [pltpu.VMEM((ROWB, 112, 768), BF), pltpu.VMEM((16, 768), F32), dma],
        table, sends_a[0], *came_a,
        memory="svvvv", micros=0,
    )
    if fast:
        swap_x = exchange(g_att_e[0], CORE)
        step.came(g_att_e[1])
        far_f = add(far_f, step.came(in_f)).astype(BF)
        mid_f = move(far_f, MIDDLE)
        second_d = step.came(second_d)
        first_d = exchange(add(g_dec[1][8:12], swap_d[8:12], second_d[:4]).astype(BF), FIRST)
        swap_x = step.came(swap_x)
        pair_x, far_x = line_add(g_att_e[1], swap_x)
        in_x = move(far_x, INWARD)
        pair_f = add(pair_f, step.came(mid_f))
        near_f = exchange(pair_f[1].astype(BF), NEAR)
        far_x = add(far_x, step.came(in_x)).astype(BF)
        mid_x = move(far_x, MIDDLE)
        first_d = step.came(first_d)
        pair_d, far_d = line_add(g_dec[1][12:], swap_d[12:], second_d[4:], first_d)
        in_d = move(far_d, INWARD)
        pair_x = add(pair_x, step.came(mid_x))
        near_x = exchange(pair_x[1].astype(BF), NEAR)
        sum_f = add(pair_f[0], step.came(near_f))
        far_d = add(far_d, step.came(in_d)).astype(BF)
        mid_d = move(far_d, MIDDLE)
        sum_x = add(pair_x[0], step.came(near_x))
        pair_d = add(pair_d, step.came(mid_d))
        near_d = exchange(pair_d[1].astype(BF), NEAR)
        sum_d = add(pair_d[0], near_d)
        sums = [sum_d, sum_f, sum_x]
        matrix_outs = unpack_grads(*sums)
        below = sums[2][None, 96:104]
    else:
        matrix_outs = []
        for number, member in enumerate(unpack_grads(g_dec[0], g_ffn_e[0], g_att_e[0])):
            if number >= 4:
                member = member.reshape(SEC, ROWB * member.shape[1], member.shape[2])
                member = lax.psum_scatter(member, "section", scatter_dimension=0, tiled=False)
            else:
                member = member.reshape(ROWB * member.shape[1], member.shape[2])
            matrix_outs.append(lax.psum_scatter(member, "dp", scatter_dimension=0, tiled=True).astype(F32))
        below = g_att_e[0][:, 96:104].astype(F32)
    vector_outs = [
        spread(member)
        for member in (
            below[:, :, :24], below[:, :, 128:144], below[:, :2, 256:272], below[:, :1, 384:480], below[:, :1, 512:576]
        )
    ]
    if not fast:
        vector_outs = [lax.psum_scatter(member, "dp", scatter_dimension=1, tiled=True) for member in vector_outs]
    enc, dec_first, dec_last, enc_u, dec_u = vector_outs
    dec_all = jnp.concatenate([dec_first, dec_last], axis=0)
    return (block_out, input_grad, *matrix_outs, enc[:2], enc[2:], enc_u[0], dec_all[:2], dec_all[2:], dec_u[0])


def solution(mesh):
    matrix, wide, line = P("dp", "section"), P(None, ("section", "dp")), P(("section", "dp"))
    image = P(("section", "dp"), None, None)
    vectors = (wide, wide, line, wide, wide, line)
    return jax.shard_map(
        shards,
        mesh=mesh,
        in_specs=(image, image, P(("section", "dp"), None), P()) + (matrix,) * 9 + vectors,
        out_specs=(image, image) + (matrix,) * 9 + vectors,
        check_vma=False,
    )
```
